512 devices in a mesh: ctx: 16 (over z_hi, x, core), dp: 32 (over z_lo, y).
Axes of the slice: x: 4, y: 8, z: 8 (z_hi: 2, z_lo: 4; z = z_hi * 4 + z_lo), core: 2. Of those that a mesh axis runs over, the one named last changes fastest.
Arguments:
- upstream: bfloat16 [4096, 2, 4096], P('ctx', None, 'dp'), may hold values from -6 to 6
- gate_value: bfloat16 [4096, 2, 4096], P('ctx', None, 'dp'), may hold values from -2 to 2
- conv_input: bfloat16 [4096, 2, 4096], P('ctx', None, 'dp'), may hold values from -2 to 2
- filters: float32 [32, 128, 4096], P(None, 'ctx', 'dp'), may hold values from -1 to 1
- skip_gain: float32 [4096], P('dp'), may hold values from 0.25 to 2
Outputs:
- input_grad: bfloat16 [4096, 2, 4096], P('ctx', None, 'dp')
- filter_grad: float32 [32, 128, 4096], P(None, 'ctx', 'dp')
The draws below stay inside these ranges and needn't reach their ends.
All inputs are finite; a program needn't handle non-finite values.
Results may differ from the reference program's by a relative error of at most 0.0049.
Values may be sent and summed in bfloat16 or wider, within the bound.
A program may use at most 64 MiB of HBM per device.

```python
import math
import jax
import jax.numpy as jnp
from jax import lax

FEATURE_WIDTH = 4096
SEQS = 2
TIME_STEPS = 4096
GROUP_CH = 128


def draw_filters(key, part):
    key = jax.random.fold_in(key, 11)
    extent_seed, spike_seed, zeroing_seed, jitter_seed = jax.random.split(key, 4)
    kernel_shift_number = jnp.arange(TIME_STEPS, dtype=jnp.float32)[None, :]
    log_low = math.log(30.0)
    log_high = math.log(TIME_STEPS * 4.0)
    reach_len = jnp.exp(jax.random.uniform(extent_seed, (FEATURE_WIDTH, 1), jnp.float32, log_low, log_high))
    spike_offset = jax.random.randint(spike_seed, (FEATURE_WIDTH, 3), 1, TIME_STEPS).astype(jnp.float32)
    spike_zeroing = jax.random.uniform(zeroing_seed, (FEATURE_WIDTH, 3), jnp.float32, 0.2, 0.5)
    fading_profile = jnp.exp(-kernel_shift_number / reach_len)
    for spike_site in range(3):
        surviving_share = (kernel_shift_number >= spike_offset[:, spike_site:spike_site + 1]).astype(jnp.float32)
        fading_profile = fading_profile * (1.0 - spike_zeroing[:, spike_site:spike_site + 1] * surviving_share)
    noise_field = jax.random.truncated_normal(jitter_seed, -4.0, 4.0, (FEATURE_WIDTH, TIME_STEPS), jnp.float32)
    row_scale = jnp.sqrt(2.0 / (jnp.minimum(reach_len, float(TIME_STEPS)) + 2.0))
    drawn = (noise_field * fading_profile * row_scale).astype(jnp.float32)
    return drawn.reshape(FEATURE_WIDTH // GROUP_CH, GROUP_CH, TIME_STEPS)


def block_levels(own_key, shape, cuts, smallest, largest):
    def one(dim, shards_of):
        steps = jax.random.uniform(jax.random.fold_in(jax.random.fold_in(own_key, 6), dim), (shards_of,), jnp.float32, smallest / len(cuts), largest / len(cuts))
        return jnp.repeat(jnp.exp(steps), shape[dim] // shards_of).reshape((-1,) + (1,) * (len(shape) - dim - 1))

    gain = one(*cuts[0])
    for cut in cuts[1:]:
        gain = gain * one(*cut)
    return gain


def scatter_about(stream_key, dims, width, reach, cuts=(), kind=jnp.bfloat16):
    factor_of = block_levels(stream_key, dims, cuts, -0.22, 0.18) if cuts else 1.0
    entries = jax.random.normal(stream_key, dims, jnp.float32) * width * factor_of
    return jnp.minimum(jnp.maximum(entries, -reach), reach).astype(kind)


def setup_inputs(seed: int = 0) -> dict:
    key_of = jax.random.split(jax.random.key(seed), 6)
    upstream = scatter_about(key_of[0], (TIME_STEPS, SEQS, FEATURE_WIDTH), 1.0, 6.0, ((0, 16), (2, 32)))
    gate_value = scatter_about(key_of[1], (TIME_STEPS, SEQS, FEATURE_WIDTH), 0.35, 2.0, ((0, 16), (2, 32)))
    conv_input = scatter_about(key_of[2], (TIME_STEPS, SEQS, FEATURE_WIDTH), 0.35, 2.0, ((0, 16), (2, 32)))
    filters = draw_filters(jax.random.fold_in(key_of[5], 71), 0)
    skip_gain = jnp.clip(0.25 + 1.75 * jax.random.uniform(key_of[4], (FEATURE_WIDTH,), jnp.float32) ** block_levels(key_of[4], (FEATURE_WIDTH,), ((0, 32),), -0.2, 0.2), 0.25, 2.0)
    return {"upstream": upstream, "gate_value": gate_value, "conv_input": conv_input, "filters": filters, "skip_gain": skip_gain}


def reference(upstream, gate_value, conv_input, filters, skip_gain):
    padded = 2 * TIME_STEPS
    width_block = min(FEATURE_WIDTH, 64)
    flat_filters = filters.reshape(FEATURE_WIDTH, TIME_STEPS)

    def one_block(first_col):
        grad_part = lax.dynamic_slice_in_dim(upstream, first_col, width_block, 2).astype(jnp.float32)
        gate_part = lax.dynamic_slice_in_dim(gate_value, first_col, width_block, 2).astype(jnp.float32)
        gate_rounded = lax.optimization_barrier((grad_part * gate_part).astype(jnp.bfloat16))
        gate_grad = gate_rounded.astype(jnp.float32)
        input_part = lax.dynamic_slice_in_dim(conv_input, first_col, width_block, 2).astype(jnp.float32)
        filt_part = lax.dynamic_slice_in_dim(flat_filters, first_col, width_block, 0)
        gain_part = lax.dynamic_slice_in_dim(skip_gain, first_col, width_block, 0)
        grad_spec = jnp.fft.rfft(gate_grad, n=padded, axis=0)
        input_spec = jnp.fft.rfft(input_part, n=padded, axis=0)
        filt_spec = jnp.fft.rfft(filt_part.T, n=padded, axis=0)
        back_sum = jnp.fft.irfft(grad_spec * jnp.conj(filt_spec)[:, None, :], n=padded, axis=0)[:TIME_STEPS]
        block_grad = (back_sum + gain_part * gate_grad).astype(jnp.bfloat16)
        cross_spec = jnp.sum(grad_spec * jnp.conj(input_spec), axis=1)
        block_filter = (jnp.fft.irfft(cross_spec, n=padded, axis=0)[:TIME_STEPS] / SEQS).T
        return block_grad, block_filter.astype(jnp.float32)

    starts = jnp.arange(FEATURE_WIDTH // width_block, dtype=jnp.int32) * width_block
    grad_blocks, filter_blocks = lax.map(one_block, starts)
    input_grad = jnp.transpose(grad_blocks, (1, 2, 0, 3)).reshape(TIME_STEPS, SEQS, FEATURE_WIDTH)
    filter_grad = filter_blocks.reshape(FEATURE_WIDTH // GROUP_CH, GROUP_CH, TIME_STEPS)
    return input_grad, filter_grad
```

```python
import functools

import jax
import jax.numpy as jnp
from jax import lax
from jax.experimental import pallas as pl
from jax.experimental.pallas import tpu as pltpu
from jax.sharding import PartitionSpec as P

MESH = pl.DeviceIdType.MESH
F32 = jnp.float32
BF16 = jnp.bfloat16

SPAN = 512
HOP = 16
LANES = 128
OWN = 8
SEQ = 2


def lane_index(shape):
    return lax.broadcasted_iota(jnp.int32, shape, len(shape) - 1)


def row_index(shape):
    return lax.broadcasted_iota(jnp.int32, shape, len(shape) - 2)


def swap_groups(blocks):
    blocks = list(blocks)
    lane = lane_index((HOP, LANES)) // HOP
    for bit in (1, 2, 4):
        upper = (lane & bit) != 0
        for r in range(8):
            if r & bit:
                continue
            low, high = blocks[r], blocks[r | bit]
            blocks[r] = jnp.where(upper, pltpu.roll(high, HOP * bit, 1), low)
            blocks[r | bit] = jnp.where(upper, high, pltpu.roll(low, LANES - HOP * bit, 1))
    return blocks


def spread_rows(wide_ref, send_ref):
    halves = []
    for s in range(SEQ):
        part = wide_ref[pl.ds(s, 256, stride=2), :]
        halves.append(part.T.reshape(16, OWN, 256))
    send_ref[...] = jnp.concatenate(halves, axis=1).astype(BF16)


def build_toeplitz(hwide_ref, toep_ref, c):
    tiles = [hwide_ref[pl.ds(OWN * h + c, 8, stride=32), :] for h in range(4)]
    before = jnp.where(row_index((8, LANES)) == 0, 0.0, pltpu.roll(tiles[3], 1, 0))
    tiles = [before] + tiles
    keep = lane_index((HOP, LANES)) >= row_index((HOP, LANES))
    for q in range(8):
        turned = [
            pltpu.roll(jnp.broadcast_to(tile[q : q + 1, :], (HOP, LANES)), 0, 1, stride=1, stride_axis=0)
            for tile in tiles
        ]
        rows = [jnp.where(keep, turned[h + 1], turned[h]) for h in range(4)]
        toep_ref[c, q * HOP : (q + 1) * HOP, :] = jnp.concatenate(rows, axis=1).astype(BF16)


def own_rows(wide_ref, c):
    seqs = []
    for s in range(SEQ):
        seqs.append(
            jnp.concatenate(
                [
                    wide_ref[v, pl.ds(h * 16 + s * OWN + c, 8, stride=32), :]
                    for h in range(2)
                    for v in range(2)
                ],
                axis=1,
            )
        )
    return jnp.concatenate(seqs, axis=0)


def build_windows(gwide_ref, win_ref, c):
    here = own_rows(gwide_ref, c)
    after = pltpu.roll(here, 15, 0)
    after = jnp.where(row_index((16, SPAN)) % 8 == 7, 0.0, after)
    both = jnp.concatenate([here, after], axis=1)
    for r in range(8):
        turned = both if r == 0 else pltpu.roll(both, 2 * SPAN - HOP * r, 1)
        for jt in range(4):
            j = 8 * jt + r
            win_ref[c, j * 16 : (j + 1) * 16, :] = turned[:, LANES * jt : LANES * jt + SPAN].astype(BF16)


def back_rows(toep_ref, win_ref, yall_ref, c):
    out = lax.dot_general(
        toep_ref[c], win_ref[c], (((1,), (1,)), ((), ())), preferred_element_type=F32
    )
    group = lane_index((HOP, LANES)) % 8
    cols = []
    for n in range(4):
        tile = out[:, n * LANES : (n + 1) * LANES]
        total = tile[0:HOP]
        for q in range(1, 8):
            turned = pltpu.roll(tile[q * HOP : (q + 1) * HOP], LANES - q, 1)
            total = total + jnp.where(group < 8 - q, turned, 0.0)
        cols.append(total)
    yall_ref[pl.ds(pl.multiple_of(c * HOP, HOP), HOP), :] = jnp.concatenate(cols, axis=1)


def finish_back(yall_ref, gwide_ref, gain_ref, first_gain, ywide_ref):
    cols = []
    for n in range(4):
        turned = yall_ref[:, n * LANES : (n + 1) * LANES].T
        cols.append(swap_groups([turned[HOP * r : HOP * (r + 1)] for r in range(8)]))
    for c in range(OWN):
        rows = jnp.concatenate([cols[n][c] for n in range(4)], axis=1)
        rows = rows + gain_ref[first_gain + c] * own_rows(gwide_ref, c)
        for s in range(SEQ):
            for h in range(2):
                for v in range(2):
                    n = 2 * h + v
                    ywide_ref[v, pl.ds(h * 16 + s * OWN + c, 8, stride=32), :] = rows[
                        8 * s : 8 * s + 8, n * LANES : (n + 1) * LANES
                    ]


def turn_inputs(xwide_ref, xall_ref):
    rows = [own_rows(xwide_ref, c) for c in range(OWN)]
    for n in range(4):
        blocks = swap_groups([row[:, n * LANES : (n + 1) * LANES] for row in rows])
        xall_ref[:, n * LANES : (n + 1) * LANES] = jnp.concatenate(blocks, axis=0).T


def filter_rows(xall_ref, xs_ref, win_ref, dwide_ref, c):
    keep = (lane_index((8, LANES)) % 8) >= row_index((8, LANES))
    for pair in range(8):
        rows = []
        for a in (2 * pair, 2 * pair + 1):
            line = xall_ref[pl.ds(c * HOP + a, 1), :]
            tiles = []
            for n in range(4):
                wide = jnp.broadcast_to(line[:, n * LANES : (n + 1) * LANES], (8, LANES))
                turned = pltpu.roll(wide, 0, 1, stride=1, stride_axis=0)
                tiles.append(jnp.where(keep, turned, 0.0))
            rows.append(jnp.concatenate(tiles, axis=1))
        xs_ref[pair * 16 : (pair + 1) * 16, :] = jnp.concatenate(rows, axis=0).astype(BF16)
    out = jnp.dot(xs_ref[...], win_ref[c], preferred_element_type=F32)
    lane = lane_index((8, LANES))
    sums = [out[0:8, n * LANES : (n + 1) * LANES] for n in range(4)]
    wrapped = jnp.zeros((8, LANES), F32)
    for a in range(1, HOP):
        turned = [
            pltpu.roll(out[8 * a : 8 * a + 8, n * LANES : (n + 1) * LANES], LANES - a, 1) for n in range(4)
        ]
        inside = lane < LANES - a
        for n in range(3):
            sums[n] = sums[n] + jnp.where(inside, turned[n], turned[n + 1])
        sums[3] = sums[3] + jnp.where(inside, turned[3], 0.0)
        wrapped = wrapped + jnp.where(inside, 0.0, turned[0])
    wrapped = jnp.where(row_index((8, LANES)) == 7, 0.0, pltpu.roll(wrapped, 7, 0))
    sums[3] = sums[3] + wrapped
    for h in range(4):
        dwide_ref[pl.ds(OWN * h + c, 8, stride=32), :] = sums[h] * (1.0 / SEQ)


def widen(ref, wide_ref):
    for v in range(2):
        wide_ref[v] = ref[:, :, v * LANES : (v + 1) * LANES].astype(F32).reshape(256, LANES)


def kernel(
    n_ctx, n_dp,
    up_ref, gate_ref, in_ref, filt_ref, gain_ref,
    out_ref, grad_ref,
    wide, gsend, xsend, grecv, xrecv, hrecv, gwide, xwide, toep, win, yall, ysend, yrecv, xall, xs, dsend,
    h_send_sem, h_recv_sem, g_send_sem, g_recv_sem, x_send_sem, x_recv_sem,
    y_send_sem, y_recv_sem, d_send_sem, d_recv_sem,
):
    me_ctx = lax.axis_index("ctx")
    me_dp = lax.axis_index("dp")

    def over_ctx(step):
        peer = lax.rem(me_ctx + step, n_ctx)
        return peer, {"ctx": peer, "dp": me_dp}

    def over_dp(step):
        peer = lax.rem(me_dp + step, n_dp)
        return peer, {"ctx": me_ctx, "dp": peer}

    barrier = pltpu.get_barrier_semaphore()

    @pl.loop(1, n_ctx)
    def _(step):
        pl.semaphore_signal(barrier, inc=1, device_id=over_ctx(step)[1], device_id_type=MESH)

    @pl.loop(1, n_dp)
    def _(step):
        pl.semaphore_signal(barrier, inc=1, device_id=over_dp(step)[1], device_id_type=MESH)

    def scatter(count, over, me, src, dst, send_sem, recv_sem):
        own = pltpu.make_async_copy(src.at[me], dst.at[me], recv_sem)
        own.start()

        @pl.loop(1, count)
        def _(step):
            peer, where = over(step)
            pltpu.make_async_remote_copy(
                src_ref=src.at[peer], dst_ref=dst.at[me], send_sem=send_sem, recv_sem=recv_sem,
                device_id=where, device_id_type=MESH,
            ).start()

    def arrive(dst, sem):
        pltpu.make_async_copy(dst, dst, sem).wait()

    def sent(count, src, sem):
        part = src.at[pl.ds(0, count - 1)]
        pltpu.make_async_copy(part, part, sem).wait()

    wide[...] = (up_ref[...].astype(F32) * gate_ref[...].astype(F32)).astype(BF16).astype(F32)
    spread_rows(wide, gsend)

    pl.semaphore_wait(barrier, n_ctx + n_dp - 2)
    scatter(n_dp, over_dp, me_dp, filt_ref, hrecv, h_send_sem, h_recv_sem)
    scatter(n_ctx, over_ctx, me_ctx, gsend, grecv, g_send_sem, g_recv_sem)
    wide[...] = in_ref[...].astype(F32)
    spread_rows(wide, xsend)
    scatter(n_ctx, over_ctx, me_ctx, xsend, xrecv, x_send_sem, x_recv_sem)

    arrive(hrecv, h_recv_sem)
    hwide = hrecv.reshape(n_dp * OWN, LANES)

    @pl.loop(0, OWN)
    def _(c):
        build_toeplitz(hwide, toep, c)

    arrive(grecv, g_recv_sem)
    widen(grecv, gwide)

    @pl.loop(0, OWN)
    def _(c):
        build_windows(gwide, win, c)
        back_rows(toep, win, yall, c)

    finish_back(yall, gwide, gain_ref, me_ctx * OWN, xwide)
    for v in range(2):
        ysend[:, :, v * LANES : (v + 1) * LANES] = xwide[v].reshape(16, 16, LANES).astype(BF16)
    scatter(n_ctx, over_ctx, me_ctx, ysend, yrecv, y_send_sem, y_recv_sem)

    arrive(xrecv, x_recv_sem)
    widen(xrecv, xwide)
    turn_inputs(xwide, xall)
    dwide = dsend.reshape(n_dp * OWN, LANES)

    @pl.loop(0, OWN)
    def _(c):
        filter_rows(xall, xs, win, dwide, c)

    scatter(n_dp, over_dp, me_dp, dsend, grad_ref, d_send_sem, d_recv_sem)

    arrive(yrecv, y_recv_sem)
    back = yrecv[...].astype(F32)
    for s in range(SEQ):
        wide[pl.ds(s, 256, stride=2), :] = back[:, s * OWN : (s + 1) * OWN, :].reshape(16 * OWN, 256).T
    out_ref[...] = wide[...].astype(BF16)

    arrive(grad_ref, d_recv_sem)
    sent(n_dp, filt_ref, h_send_sem)
    sent(n_ctx, gsend, g_send_sem)
    sent(n_ctx, xsend, x_send_sem)
    sent(n_ctx, ysend, y_send_sem)
    sent(n_dp, dsend, d_send_sem)


def body(upstream, gate_value, conv_input, filters, skip_gain):
    n_ctx = lax.axis_size("ctx")
    n_dp = lax.axis_size("dp")
    rows = upstream.shape[0] * upstream.shape[1]
    width = upstream.shape[2]
    vmem = pl.BlockSpec(memory_space=pltpu.VMEM)
    block = (16, 16, 256)
    back, grads = pl.pallas_call(
        functools.partial(kernel, n_ctx, n_dp),
        out_shape=(
            jax.ShapeDtypeStruct((rows, width), BF16),
            jax.ShapeDtypeStruct(filters.shape, F32),
        ),
        in_specs=[vmem, vmem, vmem, pl.BlockSpec(memory_space=pltpu.VMEM), pl.BlockSpec(memory_space=pltpu.SMEM)],
        out_specs=(vmem, vmem),
        scratch_shapes=[
            pltpu.VMEM((rows, width), F32),
            pltpu.VMEM(block, BF16),
            pltpu.VMEM(block, BF16),
            pltpu.VMEM(block, BF16),
            pltpu.VMEM(block, BF16),
            pltpu.VMEM(filters.shape, F32),
            pltpu.VMEM((2, 256, LANES), F32),
            pltpu.VMEM((2, 256, LANES), F32),
            pltpu.VMEM((OWN, 8 * HOP, SPAN), BF16),
            pltpu.VMEM((OWN, SPAN, SPAN), BF16),
            pltpu.VMEM((OWN * HOP, SPAN), F32),
            pltpu.VMEM(block, BF16),
            pltpu.VMEM(block, BF16),
            pltpu.VMEM((OWN * HOP, SPAN), F32),
            pltpu.VMEM((8 * HOP, SPAN), BF16),
            pltpu.VMEM(filters.shape, F32),
        ]
        + [pltpu.SemaphoreType.DMA] * 10,
        compiler_params=pltpu.CompilerParams(
            collective_id=0, has_side_effects=True, vmem_limit_bytes=32 * 1024 * 1024
        ),
    )(
        upstream.reshape(rows, width),
        gate_value.reshape(rows, width),
        conv_input.reshape(rows, width),
        filters,
        skip_gain,
    )
    return back.reshape(upstream.shape), grads


def solution(mesh):
    in_specs = (
        P("ctx", None, "dp"),
        P("ctx", None, "dp"),
        P("ctx", None, "dp"),
        P(None, "ctx", "dp"),
        P("dp"),
    )
    out_specs = (P("ctx", None, "dp"), P(None, "ctx", "dp"))
    return jax.shard_map(body, mesh=mesh, in_specs=in_specs, out_specs=out_specs, check_vma=False)
```

```python
import functools

import jax
import jax.numpy as jnp
from jax import lax
from jax.experimental import pallas as pl
from jax.experimental.pallas import tpu as pltpu
from jax.sharding import PartitionSpec as P

MESH = pl.DeviceIdType.MESH
F32 = jnp.float32
BF16 = jnp.bfloat16

SPAN = 512
HOP = 16
LANES = 128
OWN = 8
SEQ = 2


def lane_index(shape):
    return lax.broadcasted_iota(jnp.int32, shape, len(shape) - 1)


def row_index(shape):
    return lax.broadcasted_iota(jnp.int32, shape, len(shape) - 2)


def swap_groups(blocks):
    blocks = list(blocks)
    lane = lane_index((HOP, LANES)) // HOP
    for bit in (1, 2, 4):
        upper = (lane & bit) != 0
        for r in range(8):
            if r & bit:
                continue
            low, high = blocks[r], blocks[r | bit]
            blocks[r] = jnp.where(upper, pltpu.roll(high, HOP * bit, 1), low)
            blocks[r | bit] = jnp.where(upper, high, pltpu.roll(low, LANES - HOP * bit, 1))
    return blocks


def spread_rows(wide_ref, send_ref):
    halves = []
    for s in range(SEQ):
        part = wide_ref[pl.ds(s, 256, stride=2), :]
        halves.append(part.T.reshape(16, OWN, 256))
    send_ref[...] = jnp.concatenate(halves, axis=1).astype(BF16)


def build_toeplitz(hwide_ref, toep_ref, c):
    tiles = [hwide_ref[pl.ds(OWN * h + c, 8, stride=32), :] for h in range(4)]
    before = jnp.where(row_index((8, LANES)) == 0, 0.0, pltpu.roll(tiles[3], 1, 0))
    tiles = [before] + tiles
    keep = lane_index((HOP, LANES)) >= row_index((HOP, LANES))
    for q in range(8):
        turned = [
            pltpu.roll(jnp.broadcast_to(tile[q : q + 1, :], (HOP, LANES)), 0, 1, stride=1, stride_axis=0)
            for tile in tiles
        ]
        rows = [jnp.where(keep, turned[h + 1], turned[h]) for h in range(4)]
        toep_ref[c, q * HOP : (q + 1) * HOP, :] = jnp.concatenate(rows, axis=1).astype(BF16)


def own_rows(wide_ref, c):
    seqs = []
    for s in range(SEQ):
        seqs.append(
            jnp.concatenate(
                [
                    wide_ref[v, pl.ds(h * 16 + s * OWN + c, 8, stride=32), :]
                    for h in range(2)
                    for v in range(2)
                ],
                axis=1,
            )
        )
    return jnp.concatenate(seqs, axis=0)


def build_windows(gwide_ref, win_ref, c):
    here = own_rows(gwide_ref, c)
    after = pltpu.roll(here, 15, 0)
    after = jnp.where(row_index((16, SPAN)) % 8 == 7, 0.0, after)
    both = jnp.concatenate([here, after], axis=1)
    for r in range(8):
        turned = both if r == 0 else pltpu.roll(both, 2 * SPAN - HOP * r, 1)
        for jt in range(4):
            j = 8 * jt + r
            win_ref[c, j * 16 : (j + 1) * 16, :] = turned[:, LANES * jt : LANES * jt + SPAN].astype(BF16)


def back_rows(toep_ref, win_ref, yall_ref, c):
    out = lax.dot_general(
        toep_ref[c], win_ref[c], (((1,), (1,)), ((), ())), preferred_element_type=F32
    )
    group = lane_index((HOP, LANES)) % 8
    cols = []
    for n in range(4):
        tile = out[:, n * LANES : (n + 1) * LANES]
        total = tile[0:HOP]
        for q in range(1, 8):
            turned = pltpu.roll(tile[q * HOP : (q + 1) * HOP], LANES - q, 1)
            total = total + jnp.where(group < 8 - q, turned, 0.0)
        cols.append(total)
    yall_ref[pl.ds(pl.multiple_of(c * HOP, HOP), HOP), :] = jnp.concatenate(cols, axis=1)


def finish_back(yall_ref, gwide_ref, gain_ref, first_gain, ywide_ref):
    cols = []
    for n in range(4):
        turned = yall_ref[:, n * LANES : (n + 1) * LANES].T
        cols.append(swap_groups([turned[HOP * r : HOP * (r + 1)] for r in range(8)]))
    for c in range(OWN):
        rows = jnp.concatenate([cols[n][c] for n in range(4)], axis=1)
        rows = rows + gain_ref[first_gain + c] * own_rows(gwide_ref, c)
        for s in range(SEQ):
            for h in range(2):
                for v in range(2):
                    n = 2 * h + v
                    ywide_ref[v, pl.ds(h * 16 + s * OWN + c, 8, stride=32), :] = rows[
                        8 * s : 8 * s + 8, n * LANES : (n + 1) * LANES
                    ]


def turn_inputs(xwide_ref, xall_ref):
    rows = [own_rows(xwide_ref, c) for c in range(OWN)]
    for n in range(4):
        blocks = swap_groups([row[:, n * LANES : (n + 1) * LANES] for row in rows])
        xall_ref[:, n * LANES : (n + 1) * LANES] = jnp.concatenate(blocks, axis=0).T


def filter_rows(xall_ref, xs_ref, win_ref, dwide_ref, c):
    keep = (lane_index((8, LANES)) % 8) >= row_index((8, LANES))
    for pair in range(8):
        rows = []
        for a in (2 * pair, 2 * pair + 1):
            line = xall_ref[pl.ds(c * HOP + a, 1), :]
            tiles = []
            for n in range(4):
                wide = jnp.broadcast_to(line[:, n * LANES : (n + 1) * LANES], (8, LANES))
                turned = pltpu.roll(wide, 0, 1, stride=1, stride_axis=0)
                tiles.append(jnp.where(keep, turned, 0.0))
            rows.append(jnp.concatenate(tiles, axis=1))
        xs_ref[pair * 16 : (pair + 1) * 16, :] = jnp.concatenate(rows, axis=0).astype(BF16)
    out = jnp.dot(xs_ref[...], win_ref[c], preferred_element_type=F32)
    lane = lane_index((8, LANES))
    sums = [out[0:8, n * LANES : (n + 1) * LANES] for n in range(4)]
    wrapped = jnp.zeros((8, LANES), F32)
    for a in range(1, HOP):
        turned = [
            pltpu.roll(out[8 * a : 8 * a + 8, n * LANES : (n + 1) * LANES], LANES - a, 1) for n in range(4)
        ]
        inside = lane < LANES - a
        for n in range(3):
            sums[n] = sums[n] + jnp.where(inside, turned[n], turned[n + 1])
        sums[3] = sums[3] + jnp.where(inside, turned[3], 0.0)
        wrapped = wrapped + jnp.where(inside, 0.0, turned[0])
    wrapped = jnp.where(row_index((8, LANES)) == 7, 0.0, pltpu.roll(wrapped, 7, 0))
    sums[3] = sums[3] + wrapped
    for h in range(4):
        dwide_ref[pl.ds(OWN * h + c, 8, stride=32), :] = sums[h] * (1.0 / SEQ)


def widen(ref, wide_ref):
    for v in range(2):
        wide_ref[v] = ref[:, :, v * LANES : (v + 1) * LANES].astype(F32).reshape(256, LANES)


def kernel(
    n_ctx, n_dp,
    up_ref, gate_ref, in_ref, filt_ref, gain_ref,
    yrecv, drecv,
    up, gate, raw, filt, gain, wide, gsend, xsend, hsend, grecv, xrecv, hrecv, gwide, xwide, hwide, toep, win,
    yall, ysend, xall, xs, dwide, dsend,
    load_sem,
    h_send_sem, h_recv_sem, g_send_sem, g_recv_sem, x_send_sem, x_recv_sem,
    y_send_sem, y_recv_sem, d_send_sem, d_recv_sem,
):
    me_ctx = lax.axis_index("ctx")
    me_dp = lax.axis_index("dp")
    half = n_ctx // 2
    me_hi = me_ctx // half
    me_lo = lax.rem(me_ctx, half)

    def far_ctx(step):
        peer = (1 - me_hi) * half + lax.rem(me_lo + step, half)
        return peer, {"ctx": peer, "dp": me_dp}

    def near_ctx(step):
        peer = me_hi * half + lax.rem(me_lo + step, half)
        return peer, {"ctx": peer, "dp": me_dp}

    def over_dp(step):
        peer = lax.rem(me_dp + step, n_dp)
        return peer, {"ctx": me_ctx, "dp": peer}

    loads = [
        pltpu.make_async_copy(src, dst, load_sem.at[n])
        for n, (src, dst) in enumerate(
            ((up_ref, up), (gate_ref, gate), (in_ref, raw), (filt_ref, filt), (gain_ref, gain))
        )
    ]
    for load in loads:
        load.start()

    barrier = pltpu.get_barrier_semaphore()

    def greet(first, last, over):
        @pl.loop(first, last)
        def _(step):
            pl.semaphore_signal(barrier, inc=1, device_id=over(step)[1], device_id_type=MESH)

    greet(0, half, far_ctx)
    greet(1, n_dp, over_dp)
    greet(1, half, near_ctx)

    def scatter(first, last, over, me, src, dst, send_sem, recv_sem):
        @pl.loop(first, last)
        def _(step):
            peer, where = over(step)
            pltpu.make_async_remote_copy(
                src_ref=src.at[peer], dst_ref=dst.at[me], send_sem=send_sem, recv_sem=recv_sem,
                device_id=where, device_id_type=MESH,
            ).start()

    def keep_own(me, src, dst, recv_sem):
        pltpu.make_async_copy(src.at[me], dst.at[me], recv_sem).start()

    def arrive(dst, sem):
        pltpu.make_async_copy(dst, dst, sem).wait()

    def sent(count, src, sem):
        part = src.at[pl.ds(0, count - 1)]
        pltpu.make_async_copy(part, part, sem).wait()

    loads[0].wait()
    loads[1].wait()
    wide[...] = (up[...].astype(F32) * gate[...].astype(F32)).astype(BF16).astype(F32)
    spread_rows(wide, gsend)
    loads[3].wait()
    hsend[...] = filt[...].astype(BF16)
    loads[2].wait()
    wide[...] = raw[...].astype(F32)
    spread_rows(wide, xsend)

    pl.semaphore_wait(barrier, n_ctx + n_dp - 2)
    scatter(0, half, far_ctx, me_ctx, gsend, grecv, g_send_sem, g_recv_sem)
    scatter(1, n_dp, over_dp, me_dp, hsend, hrecv, h_send_sem, h_recv_sem)
    scatter(1, half, near_ctx, me_ctx, gsend, grecv, g_send_sem, g_recv_sem)
    scatter(0, half, far_ctx, me_ctx, xsend, xrecv, x_send_sem, x_recv_sem)
    scatter(1, half, near_ctx, me_ctx, xsend, xrecv, x_send_sem, x_recv_sem)
    keep_own(me_dp, hsend, hrecv, h_recv_sem)
    keep_own(me_ctx, gsend, grecv, g_recv_sem)
    keep_own(me_ctx, xsend, xrecv, x_recv_sem)
    loads[4].wait()

    arrive(hrecv, h_recv_sem)
    hwide[...] = hrecv[...].astype(F32).reshape(n_dp * OWN, LANES)
    for c in range(OWN):
        build_toeplitz(hwide, toep, c)

    arrive(grecv, g_recv_sem)
    widen(grecv, gwide)
    for c in range(OWN):
        build_windows(gwide, win, c)
    for c in range(OWN):
        back_rows(toep, win, yall, c)
    finish_back(yall, gwide, gain, me_ctx * OWN, xwide)
    for v in range(2):
        ysend[:, :, v * LANES : (v + 1) * LANES] = xwide[v].reshape(16, 16, LANES).astype(BF16)
    scatter(0, half, far_ctx, me_ctx, ysend, yrecv, y_send_sem, y_recv_sem)
    scatter(1, half, near_ctx, me_ctx, ysend, yrecv, y_send_sem, y_recv_sem)
    keep_own(me_ctx, ysend, yrecv, y_recv_sem)

    arrive(xrecv, x_recv_sem)
    widen(xrecv, xwide)
    turn_inputs(xwide, xall)
    for c in range(OWN):
        filter_rows(xall, xs, win, dwide, c)
    dsend[...] = dwide[...].reshape(n_dp, OWN, LANES).astype(BF16)
    scatter(1, n_dp, over_dp, me_dp, dsend, drecv, d_send_sem, d_recv_sem)
    keep_own(me_dp, dsend, drecv, d_recv_sem)

    sent(n_dp, hsend, h_send_sem)
    sent(n_ctx, gsend, g_send_sem)
    sent(n_ctx, xsend, x_send_sem)
    sent(n_ctx, ysend, y_send_sem)
    sent(n_dp, dsend, d_send_sem)
    arrive(yrecv, y_recv_sem)
    arrive(drecv, d_recv_sem)


def finish_kernel(yrecv, drecv, out_ref, grad_ref, y_in, d_in, wide, out, grad, load_sem):
    loads = [
        pltpu.make_async_copy(src, dst, load_sem.at[n])
        for n, (src, dst) in enumerate(((drecv, d_in), (yrecv, y_in)))
    ]
    stores = [
        pltpu.make_async_copy(src, dst, load_sem.at[n])
        for n, (src, dst) in enumerate(((grad, grad_ref), (out, out_ref)))
    ]
    for load in loads:
        load.start()
    loads[0].wait()
    grad[...] = d_in[...].astype(F32)
    stores[0].start()
    loads[1].wait()
    back = y_in[...].astype(F32)
    for s in range(SEQ):
        wide[pl.ds(s, 256, stride=2), :] = back[:, s * OWN : (s + 1) * OWN, :].reshape(16 * OWN, 256).T
    out[...] = wide[...].astype(BF16)
    stores[1].start()
    for store in stores:
        store.wait()


def body(upstream, gate_value, conv_input, filters, skip_gain):
    n_ctx = lax.axis_size("ctx")
    n_dp = lax.axis_size("dp")
    rows = upstream.shape[0] * upstream.shape[1]
    width = upstream.shape[2]
    block = (16, 16, 256)
    hbm = pl.BlockSpec(memory_space=pltpu.HBM)
    grant = 56 * 1024 * 1024
    back, grads = pl.pallas_call(
        functools.partial(kernel, n_ctx, n_dp),
        out_shape=(jax.ShapeDtypeStruct(block, BF16), jax.ShapeDtypeStruct(filters.shape, BF16)),
        in_specs=[hbm] * 5,
        out_specs=[hbm] * 2,
        scratch_shapes=[
            pltpu.VMEM((rows, width), BF16),
            pltpu.VMEM((rows, width), BF16),
            pltpu.VMEM((rows, width), BF16),
            pltpu.VMEM(filters.shape, F32),
            pltpu.SMEM(skip_gain.shape, F32),
            pltpu.VMEM((rows, width), F32),
            pltpu.VMEM(block, BF16),
            pltpu.VMEM(block, BF16),
            pltpu.VMEM(filters.shape, BF16),
            pltpu.VMEM(block, BF16),
            pltpu.VMEM(block, BF16),
            pltpu.VMEM(filters.shape, BF16),
            pltpu.VMEM((2, 256, LANES), F32),
            pltpu.VMEM((2, 256, LANES), F32),
            pltpu.VMEM((n_dp * OWN, LANES), F32),
            pltpu.VMEM((OWN, 8 * HOP, SPAN), BF16),
            pltpu.VMEM((OWN, SPAN, SPAN), BF16),
            pltpu.VMEM((OWN * HOP, SPAN), F32),
            pltpu.VMEM(block, BF16),
            pltpu.VMEM((OWN * HOP, SPAN), F32),
            pltpu.VMEM((8 * HOP, SPAN), BF16),
            pltpu.VMEM((n_dp * OWN, LANES), F32),
            pltpu.VMEM(filters.shape, BF16),
        ]
        + [pltpu.SemaphoreType.DMA((5,))]
        + [pltpu.SemaphoreType.DMA] * 10,
        compiler_params=pltpu.CompilerParams(collective_id=0, has_side_effects=True, vmem_limit_bytes=grant),
    )(
        upstream.reshape(rows, width),
        gate_value.reshape(rows, width),
        conv_input.reshape(rows, width),
        filters,
        skip_gain,
    )
    out, grad = pl.pallas_call(
        finish_kernel,
        out_shape=(jax.ShapeDtypeStruct((rows, width), BF16), jax.ShapeDtypeStruct(filters.shape, F32)),
        in_specs=[hbm] * 2,
        out_specs=[hbm] * 2,
        scratch_shapes=[
            pltpu.VMEM(block, BF16),
            pltpu.VMEM(filters.shape, BF16),
            pltpu.VMEM((rows, width), F32),
            pltpu.VMEM((rows, width), BF16),
            pltpu.VMEM(filters.shape, F32),
            pltpu.SemaphoreType.DMA((2,)),
        ],
        compiler_params=pltpu.CompilerParams(vmem_limit_bytes=grant),
    )(back, grads)
    return out.reshape(upstream.shape), grad


def solution(mesh):
    in_specs = (
        P("ctx", None, "dp"),
        P("ctx", None, "dp"),
        P("ctx", None, "dp"),
        P(None, "ctx", "dp"),
        P("dp"),
    )
    out_specs = (P("ctx", None, "dp"), P(None, "ctx", "dp"))
    return jax.shard_map(body, mesh=mesh, in_specs=in_specs, out_specs=out_specs, check_vma=False)
```

```python
import functools

import jax
import jax.numpy as jnp
from jax import lax
from jax.experimental import pallas as pl
from jax.experimental.pallas import tpu as pltpu
from jax.sharding import PartitionSpec as P

MESH = pl.DeviceIdType.MESH
F32 = jnp.float32
BF16 = jnp.bfloat16

SPAN = 512
HOP = 16
LANES = 128
OWN = 8
SEQ = 2
LINE = 8


def lane_index(shape):
    return lax.broadcasted_iota(jnp.int32, shape, len(shape) - 1)


def row_index(shape):
    return lax.broadcasted_iota(jnp.int32, shape, len(shape) - 2)


def swap_groups(blocks):
    blocks = list(blocks)
    lane = lane_index((HOP, LANES)) // HOP
    for bit in (1, 2, 4):
        upper = (lane & bit) != 0
        for r in range(8):
            if r & bit:
                continue
            low, high = blocks[r], blocks[r | bit]
            blocks[r] = jnp.where(upper, pltpu.roll(high, HOP * bit, 1), low)
            blocks[r | bit] = jnp.where(upper, high, pltpu.roll(low, LANES - HOP * bit, 1))
    return blocks


def spread_rows(wide_ref, send_ref):
    halves = []
    for s in range(SEQ):
        part = wide_ref[pl.ds(s, 256, stride=2), :]
        halves.append(part.T.reshape(16, OWN, 256))
    send_ref[...] = jnp.concatenate(halves, axis=1).astype(BF16)


def build_toeplitz(hwide_ref, toep_ref, c):
    tiles = [hwide_ref[pl.ds(OWN * h + c, 8, stride=32), :] for h in range(4)]
    before = jnp.where(row_index((8, LANES)) == 0, 0.0, pltpu.roll(tiles[3], 1, 0))
    tiles = [before] + tiles
    keep = lane_index((HOP, LANES)) >= row_index((HOP, LANES))
    for q in range(8):
        turned = [
            pltpu.roll(jnp.broadcast_to(tile[q : q + 1, :], (HOP, LANES)), 0, 1, stride=1, stride_axis=0)
            for tile in tiles
        ]
        rows = [jnp.where(keep, turned[h + 1], turned[h]) for h in range(4)]
        toep_ref[c, q * HOP : (q + 1) * HOP, :] = jnp.concatenate(rows, axis=1).astype(BF16)


def own_rows(wide_ref, c):
    seqs = []
    for s in range(SEQ):
        seqs.append(
            jnp.concatenate(
                [
                    wide_ref[v, pl.ds(h * 16 + s * OWN + c, 8, stride=32), :]
                    for h in range(2)
                    for v in range(2)
                ],
                axis=1,
            )
        )
    return jnp.concatenate(seqs, axis=0)


def build_windows(gwide_ref, win_ref, c):
    here = own_rows(gwide_ref, c)
    after = pltpu.roll(here, 15, 0)
    after = jnp.where(row_index((16, SPAN)) % 8 == 7, 0.0, after)
    both = jnp.concatenate([here, after], axis=1)
    for r in range(8):
        turned = both if r == 0 else pltpu.roll(both, 2 * SPAN - HOP * r, 1)
        for jt in range(4):
            j = 8 * jt + r
            win_ref[c, j * 16 : (j + 1) * 16, :] = turned[:, LANES * jt : LANES * jt + SPAN].astype(BF16)


def back_rows(toep_ref, win_ref, yall_ref, c):
    out = lax.dot_general(
        toep_ref[c], win_ref[c], (((1,), (1,)), ((), ())), preferred_element_type=F32
    )
    group = lane_index((HOP, LANES)) % 8
    cols = []
    for n in range(4):
        tile = out[:, n * LANES : (n + 1) * LANES]
        total = tile[0:HOP]
        for q in range(1, 8):
            turned = pltpu.roll(tile[q * HOP : (q + 1) * HOP], LANES - q, 1)
            total = total + jnp.where(group < 8 - q, turned, 0.0)
        cols.append(total)
    yall_ref[pl.ds(pl.multiple_of(c * HOP, HOP), HOP), :] = jnp.concatenate(cols, axis=1)


def finish_back(yall_ref, gwide_ref, gain_ref, first_gain, ywide_ref):
    cols = []
    for n in range(4):
        turned = yall_ref[:, n * LANES : (n + 1) * LANES].T
        cols.append(swap_groups([turned[HOP * r : HOP * (r + 1)] for r in range(8)]))
    for c in range(OWN):
        rows = jnp.concatenate([cols[n][c] for n in range(4)], axis=1)
        rows = rows + gain_ref[first_gain + c] * own_rows(gwide_ref, c)
        for s in range(SEQ):
            for h in range(2):
                for v in range(2):
                    n = 2 * h + v
                    ywide_ref[v, pl.ds(h * 16 + s * OWN + c, 8, stride=32), :] = rows[
                        8 * s : 8 * s + 8, n * LANES : (n + 1) * LANES
                    ]


def turn_inputs(xwide_ref, xall_ref):
    rows = [own_rows(xwide_ref, c) for c in range(OWN)]
    for n in range(4):
        blocks = swap_groups([row[:, n * LANES : (n + 1) * LANES] for row in rows])
        xall_ref[:, n * LANES : (n + 1) * LANES] = jnp.concatenate(blocks, axis=0).T


def filter_rows(xall_ref, xs_ref, win_ref, dwide_ref, c):
    keep = (lane_index((8, LANES)) % 8) >= row_index((8, LANES))
    for pair in range(8):
        rows = []
        for a in (2 * pair, 2 * pair + 1):
            line = xall_ref[pl.ds(c * HOP + a, 1), :]
            tiles = []
            for n in range(4):
                wide = jnp.broadcast_to(line[:, n * LANES : (n + 1) * LANES], (8, LANES))
                turned = pltpu.roll(wide, 0, 1, stride=1, stride_axis=0)
                tiles.append(jnp.where(keep, turned, 0.0))
            rows.append(jnp.concatenate(tiles, axis=1))
        xs_ref[pair * 16 : (pair + 1) * 16, :] = jnp.concatenate(rows, axis=0).astype(BF16)
    out = jnp.dot(xs_ref[...], win_ref[c], preferred_element_type=F32)
    lane = lane_index((8, LANES))
    sums = [out[0:8, n * LANES : (n + 1) * LANES] for n in range(4)]
    wrapped = jnp.zeros((8, LANES), F32)
    for a in range(1, HOP):
        turned = [
            pltpu.roll(out[8 * a : 8 * a + 8, n * LANES : (n + 1) * LANES], LANES - a, 1) for n in range(4)
        ]
        inside = lane < LANES - a
        for n in range(3):
            sums[n] = sums[n] + jnp.where(inside, turned[n], turned[n + 1])
        sums[3] = sums[3] + jnp.where(inside, turned[3], 0.0)
        wrapped = wrapped + jnp.where(inside, 0.0, turned[0])
    wrapped = jnp.where(row_index((8, LANES)) == 7, 0.0, pltpu.roll(wrapped, 7, 0))
    sums[3] = sums[3] + wrapped
    for h in range(4):
        dwide_ref[pl.ds(OWN * h + c, 8, stride=32), :] = sums[h] * (1.0 / SEQ)


def widen(ref, wide_ref):
    for v in range(2):
        wide_ref[v] = ref[:, :, v * LANES : (v + 1) * LANES].astype(F32).reshape(256, LANES)


def kernel(
    n_ctx, n_dp, n_y,
    up_ref, gate_ref, in_ref, filt_ref, gain_ref,
    yrecv, drecv,
    up, gate, raw, filt, gain, wide, gsend, xsend, hsend, hpass, hturn, grecv, xrecv, hrecv, gwide, xwide, hwide, toep, win,
    yall, ywide, ysend, xall, xs, dwide, dsend,
    load_sem,
    h_send_sem, h_recv_sem, t_send_sem, t_recv_sem, g_send_sem, g_recv_sem, x_send_sem, x_recv_sem,
    y_send_sem, y_recv_sem, d_send_sem, d_recv_sem,
):
    me_ctx = lax.axis_index("ctx")
    me_dp = lax.axis_index("dp")
    half = n_ctx // 2
    me_hi = me_ctx // half
    me_lo = lax.rem(me_ctx, half)
    n_z = n_dp // n_y
    me_z = me_dp // n_y
    me_y = lax.rem(me_dp, n_y)

    def far_ctx(step):
        peer = (1 - me_hi) * half + lax.rem(me_lo + step, half)
        return peer, {"ctx": peer, "dp": me_dp}

    def near_ctx(step):
        peer = me_hi * half + lax.rem(me_lo + step, half)
        return peer, {"ctx": peer, "dp": me_dp}

    def over_dp(step):
        peer = lax.rem(me_dp + step, n_dp)
        return peer, {"ctx": me_ctx, "dp": peer}

    def over_y(step):
        peer = lax.rem(me_y + step, n_y)
        return peer, {"ctx": me_ctx, "dp": me_z * n_y + peer}

    def over_z(step):
        peer = lax.rem(me_z + step, n_z)
        return peer, {"ctx": me_ctx, "dp": peer * n_y + me_y}

    loads = [
        pltpu.make_async_copy(src, dst, load_sem.at[n])
        for n, (src, dst) in enumerate(
            ((up_ref, up), (gate_ref, gate), (in_ref, raw), (filt_ref, filt), (gain_ref, gain))
        )
    ]
    for load in loads:
        load.start()

    barrier = pltpu.get_barrier_semaphore()

    def greet(first, last, over):
        @pl.loop(first, last)
        def _(step):
            pl.semaphore_signal(barrier, inc=1, device_id=over(step)[1], device_id_type=MESH)

    greet(0, half, far_ctx)
    greet(1, n_y, over_y)
    greet(1, n_z, over_z)
    greet(1, half, near_ctx)

    def scatter(first, last, over, me, src, dst, send_sem, recv_sem):
        @pl.loop(first, last)
        def _(step):
            peer, where = over(step)
            pltpu.make_async_remote_copy(
                src_ref=src.at[peer], dst_ref=dst.at[me], send_sem=send_sem, recv_sem=recv_sem,
                device_id=where, device_id_type=MESH,
            ).start()

    def keep_own(me, src, dst, recv_sem):
        pltpu.make_async_copy(src.at[me], dst.at[me], recv_sem).start()

    def arrive(dst, sem):
        pltpu.make_async_copy(dst, dst, sem).wait()

    def sent(count, src, sem):
        part = src.at[pl.ds(0, count - 1)]
        pltpu.make_async_copy(part, part, sem).wait()

    loads[0].wait()
    loads[1].wait()
    wide[...] = (up[...].astype(F32) * gate[...].astype(F32)).astype(BF16).astype(F32)
    spread_rows(wide, gsend)
    loads[3].wait()
    lags = filt[...].reshape(n_z, n_y, OWN, LANES)
    hsend[...] = jnp.swapaxes(lags, 0, 1).reshape(n_y, n_z * OWN, LANES).astype(BF16)
    loads[2].wait()
    wide[...] = raw[...].astype(F32)
    spread_rows(wide, xsend)

    pl.semaphore_wait(barrier, n_ctx + n_y + n_z - 3)
    scatter(0, half, far_ctx, me_ctx, gsend, grecv, g_send_sem, g_recv_sem)

    @pl.when(me_hi == 1)
    def _():
        scatter(0, half, far_ctx, me_ctx, xsend, xrecv, x_send_sem, x_recv_sem)

    scatter(1, n_y, over_y, me_y, hsend, hpass, h_send_sem, h_recv_sem)
    scatter(1, half, near_ctx, me_ctx, gsend, grecv, g_send_sem, g_recv_sem)
    scatter(1, half, near_ctx, me_ctx, xsend, xrecv, x_send_sem, x_recv_sem)
    keep_own(me_y, hsend, hpass, h_recv_sem)
    keep_own(me_ctx, gsend, grecv, g_recv_sem)
    keep_own(me_ctx, xsend, xrecv, x_recv_sem)
    loads[4].wait()

    arrive(hpass, h_recv_sem)
    lags = hpass[...].astype(F32).reshape(n_y, n_z, OWN, LANES)
    hturn[...] = jnp.swapaxes(lags, 0, 1).reshape(n_z, n_y * OWN, LANES).astype(BF16)
    scatter(1, n_z, over_z, me_z, hturn, hrecv, t_send_sem, t_recv_sem)
    keep_own(me_z, hturn, hrecv, t_recv_sem)

    arrive(grecv, g_recv_sem)

    @pl.when(me_hi == 0)
    def _():
        scatter(0, half, far_ctx, me_ctx, xsend, xrecv, x_send_sem, x_recv_sem)

    widen(grecv, gwide)
    for c in range(OWN):
        build_windows(gwide, win, c)

    @pl.loop(0, 2)
    def _(turn):
        @pl.when(turn != me_hi)
        def _():
            arrive(hrecv, t_recv_sem)
            hwide[...] = hrecv[...].astype(F32).reshape(n_dp * OWN, LANES)
            for c in range(OWN):
                build_toeplitz(hwide, toep, c)

            for c in range(OWN):
                back_rows(toep, win, yall, c)
            finish_back(yall, gwide, gain, me_ctx * OWN, ywide)
            for v in range(2):
                ysend[:, :, v * LANES : (v + 1) * LANES] = ywide[v].reshape(16, 16, LANES).astype(BF16)
            scatter(0, half, far_ctx, me_ctx, ysend, yrecv, y_send_sem, y_recv_sem)
            scatter(1, half, near_ctx, me_ctx, ysend, yrecv, y_send_sem, y_recv_sem)
            keep_own(me_ctx, ysend, yrecv, y_recv_sem)

        @pl.when(turn == me_hi)
        def _():
            arrive(xrecv, x_recv_sem)
            widen(xrecv, xwide)
            turn_inputs(xwide, xall)
            for c in range(OWN):
                filter_rows(xall, xs, win, dwide, c)
            dsend[...] = dwide[...].reshape(n_dp, OWN, LANES).astype(BF16)
            scatter(1, n_dp, over_dp, me_dp, dsend, drecv, d_send_sem, d_recv_sem)
            keep_own(me_dp, dsend, drecv, d_recv_sem)

    sent(n_y, hsend, h_send_sem)
    sent(n_z, hturn, t_send_sem)
    sent(n_ctx, gsend, g_send_sem)
    sent(n_ctx, xsend, x_send_sem)
    sent(n_ctx, ysend, y_send_sem)
    sent(n_dp, dsend, d_send_sem)
    arrive(yrecv, y_recv_sem)
    arrive(drecv, d_recv_sem)


def finish_kernel(y_in, d_in, out_ref, grad_ref, wide, out, grad, store_sem):
    stores = [
        pltpu.make_async_copy(src, dst, store_sem.at[n])
        for n, (src, dst) in enumerate(((grad, grad_ref), (out, out_ref)))
    ]
    grad[...] = d_in[...].astype(F32)
    stores[0].start()
    back = y_in[...].astype(F32)
    for s in range(SEQ):
        wide[pl.ds(s, 256, stride=2), :] = back[:, s * OWN : (s + 1) * OWN, :].reshape(16 * OWN, 256).T
    out[...] = wide[...].astype(BF16)
    stores[1].start()
    for store in stores:
        store.wait()


def body(upstream, gate_value, conv_input, filters, skip_gain):
    n_ctx = lax.axis_size("ctx")
    n_dp = lax.axis_size("dp")
    n_y = LINE
    n_z = n_dp // n_y
    rows = upstream.shape[0] * upstream.shape[1]
    width = upstream.shape[2]
    block = (16, 16, 256)
    hbm = pl.BlockSpec(memory_space=pltpu.HBM)
    grant = 56 * 1024 * 1024
    back, grads = pl.pallas_call(
        functools.partial(kernel, n_ctx, n_dp, n_y),
        out_shape=(pltpu.VMEM(block, BF16), pltpu.VMEM(filters.shape, BF16)),
        in_specs=[hbm] * 5,
        out_specs=[pl.BlockSpec(memory_space=pltpu.VMEM)] * 2,
        scratch_shapes=[
            pltpu.VMEM((rows, width), BF16),
            pltpu.VMEM((rows, width), BF16),
            pltpu.VMEM((rows, width), BF16),
            pltpu.VMEM(filters.shape, F32),
            pltpu.SMEM(skip_gain.shape, F32),
            pltpu.VMEM((rows, width), F32),
            pltpu.VMEM(block, BF16),
            pltpu.VMEM(block, BF16),
            pltpu.VMEM((n_y, n_z * OWN, LANES), BF16),
            pltpu.VMEM((n_y, n_z * OWN, LANES), BF16),
            pltpu.VMEM((n_z, n_y * OWN, LANES), BF16),
            pltpu.VMEM(block, BF16),
            pltpu.VMEM(block, BF16),
            pltpu.VMEM((n_z, n_y * OWN, LANES), BF16),
            pltpu.VMEM((2, 256, LANES), F32),
            pltpu.VMEM((2, 256, LANES), F32),
            pltpu.VMEM((n_dp * OWN, LANES), F32),
            pltpu.VMEM((OWN, 8 * HOP, SPAN), BF16),
            pltpu.VMEM((OWN, SPAN, SPAN), BF16),
            pltpu.VMEM((OWN * HOP, SPAN), F32),
            pltpu.VMEM((2, 256, LANES), F32),
            pltpu.VMEM(block, BF16),
            pltpu.VMEM((OWN * HOP, SPAN), F32),
            pltpu.VMEM((8 * HOP, SPAN), BF16),
            pltpu.VMEM((n_dp * OWN, LANES), F32),
            pltpu.VMEM(filters.shape, BF16),
        ]
        + [pltpu.SemaphoreType.DMA((5,))]
        + [pltpu.SemaphoreType.DMA] * 12,
        compiler_params=pltpu.CompilerParams(collective_id=0, has_side_effects=True, vmem_limit_bytes=grant),
    )(
        upstream.reshape(rows, width),
        gate_value.reshape(rows, width),
        conv_input.reshape(rows, width),
        filters,
        skip_gain,
    )
    out, grad = pl.pallas_call(
        finish_kernel,
        out_shape=(jax.ShapeDtypeStruct((rows, width), BF16), jax.ShapeDtypeStruct(filters.shape, F32)),
        in_specs=[pl.BlockSpec(memory_space=pltpu.VMEM)] * 2,
        out_specs=[hbm] * 2,
        scratch_shapes=[
            pltpu.VMEM((rows, width), F32),
            pltpu.VMEM((rows, width), BF16),
            pltpu.VMEM(filters.shape, F32),
            pltpu.SemaphoreType.DMA((2,)),
        ],
        compiler_params=pltpu.CompilerParams(vmem_limit_bytes=16 * 1024 * 1024),
    )(back, grads)
    return out.reshape(upstream.shape), grad


def solution(mesh):
    in_specs = (
        P("ctx", None, "dp"),
        P("ctx", None, "dp"),
        P("ctx", None, "dp"),
        P(None, "ctx", "dp"),
        P("dp"),
    )
    out_specs = (P("ctx", None, "dp"), P(None, "ctx", "dp"))
    return jax.shard_map(body, mesh=mesh, in_specs=in_specs, out_specs=out_specs, check_vma=False)
```

```python
import functools

import jax
import jax.numpy as jnp
from jax import lax
from jax.experimental import pallas as pl
from jax.experimental.pallas import tpu as pltpu
from jax.sharding import PartitionSpec as P

MESH = pl.DeviceIdType.MESH
F32 = jnp.float32
BF16 = jnp.bfloat16

SPAN = 512
HOP = 16
LANES = 128
OWN = 8
SEQ = 2
LINE = 8


def lane_index(shape):
    return lax.broadcasted_iota(jnp.int32, shape, len(shape) - 1)


def row_index(shape):
    return lax.broadcasted_iota(jnp.int32, shape, len(shape) - 2)


def swap_groups(blocks):
    blocks = list(blocks)
    lane = lane_index((HOP, LANES)) // HOP
    for bit in (1, 2, 4):
        upper = (lane & bit) != 0
        for r in range(8):
            if r & bit:
                continue
            low, high = blocks[r], blocks[r | bit]
            blocks[r] = jnp.where(upper, pltpu.roll(high, HOP * bit, 1), low)
            blocks[r | bit] = jnp.where(upper, high, pltpu.roll(low, LANES - HOP * bit, 1))
    return blocks


def spread_rows(wide_ref, send_ref):
    halves = []
    for s in range(SEQ):
        part = wide_ref[pl.ds(s, 256, stride=2), :]
        halves.append(part.T.reshape(16, OWN, 256))
    send_ref[...] = jnp.concatenate(halves, axis=1).astype(BF16)


def build_toeplitz(hwide_ref, toep_ref, c):
    tiles = [hwide_ref[pl.ds(OWN * h + c, 8, stride=32), :] for h in range(4)]
    before = jnp.where(row_index((8, LANES)) == 0, 0.0, pltpu.roll(tiles[3], 1, 0))
    tiles = [before] + tiles
    keep = lane_index((HOP, LANES)) >= row_index((HOP, LANES))
    for q in range(8):
        turned = [
            pltpu.roll(jnp.broadcast_to(tile[q : q + 1, :], (HOP, LANES)), 0, 1, stride=1, stride_axis=0)
            for tile in tiles
        ]
        rows = [jnp.where(keep, turned[h + 1], turned[h]) for h in range(4)]
        toep_ref[c, q * HOP : (q + 1) * HOP, :] = jnp.concatenate(rows, axis=1).astype(BF16)


def own_rows(wide_ref, c):
    seqs = []
    for s in range(SEQ):
        seqs.append(
            jnp.concatenate(
                [
                    wide_ref[v, pl.ds(h * 16 + s * OWN + c, 8, stride=32), :]
                    for h in range(2)
                    for v in range(2)
                ],
                axis=1,
            )
        )
    return jnp.concatenate(seqs, axis=0)


def build_windows(gwide_ref, win_ref, c):
    here = own_rows(gwide_ref, c)
    after = pltpu.roll(here, 15, 0)
    after = jnp.where(row_index((16, SPAN)) % 8 == 7, 0.0, after)
    both = jnp.concatenate([here, after], axis=1)
    for r in range(8):
        turned = both if r == 0 else pltpu.roll(both, 2 * SPAN - HOP * r, 1)
        for jt in range(4):
            j = 8 * jt + r
            win_ref[c, j * 16 : (j + 1) * 16, :] = turned[:, LANES * jt : LANES * jt + SPAN].astype(BF16)


def back_rows(toep_ref, wint_ref, yall_ref, c, h):
    out = jnp.dot(toep_ref[c], wint_ref[c, :, 256 * h : 256 * h + 256], preferred_element_type=F32)
    group = lane_index((HOP, LANES)) % 8
    for n in range(2):
        tile = out[:, n * LANES : (n + 1) * LANES]
        total = tile[0:HOP]
        for q in range(1, 8):
            turned = pltpu.roll(tile[q * HOP : (q + 1) * HOP], LANES - q, 1)
            total = total + jnp.where(group < 8 - q, turned, 0.0)
        yall_ref[c * HOP : (c + 1) * HOP, 256 * h + n * LANES : 256 * h + (n + 1) * LANES] = total


def finish_back(yall_ref, gwide_ref, gain_ref, first_gain, ywide_ref, ysend_ref, h):
    cols = []
    for n in (2 * h, 2 * h + 1):
        turned = yall_ref[:, n * LANES : (n + 1) * LANES].T
        cols.append(swap_groups([turned[HOP * r : HOP * (r + 1)] for r in range(8)]))
    for c in range(OWN):
        gain = gain_ref[first_gain + c]
        for v in range(2):
            for s in range(SEQ):
                rows = cols[v][c][8 * s : 8 * s + 8]
                here = gwide_ref[v, pl.ds(h * 16 + s * OWN + c, 8, stride=32), :]
                ywide_ref[v, pl.ds(s * OWN + c, 8, stride=16), :] = rows + gain * here
    for v in range(2):
        ysend_ref[:, h, :, v * LANES : (v + 1) * LANES] = ywide_ref[v].reshape(8, 16, LANES).astype(BF16)


def turn_inputs(xwide_ref, xall_ref):
    rows = [own_rows(xwide_ref, c) for c in range(OWN)]
    for n in range(4):
        blocks = swap_groups([row[:, n * LANES : (n + 1) * LANES] for row in rows])
        xall_ref[:, n * LANES : (n + 1) * LANES] = jnp.concatenate(blocks, axis=0).T


def shift_inputs(xall_ref, xs_ref, c):
    group = lane_index((HOP, LANES)) % 8
    for n in range(4):
        tile = xall_ref[c * HOP : (c + 1) * HOP, n * LANES : (n + 1) * LANES].astype(BF16)
        for q in range(8):
            turned = tile if q == 0 else jnp.where(group >= q, pltpu.roll(tile, q, 1), jnp.zeros_like(tile))
            xs_ref[c, q * HOP : (q + 1) * HOP, n * LANES : (n + 1) * LANES] = turned


def filter_rows(xs_ref, win_ref, sums_ref, dwide_ref, c):
    out = jnp.dot(xs_ref[c], win_ref[c], preferred_element_type=F32)
    for n in range(4):
        sums_ref[c, n] = out[:, n * LANES : (n + 1) * LANES]
    lane = lane_index((8, LANES))
    rows = [[sums_ref[c, n, pl.ds(a, 8, stride=HOP), :] for n in range(4)] for a in range(HOP)]
    sums = rows[0]
    wrapped = jnp.zeros((8, LANES), F32)
    for a in range(1, HOP):
        turned = [pltpu.roll(row, LANES - a, 1) for row in rows[a]]
        inside = lane < LANES - a
        for n in range(3):
            sums[n] = sums[n] + jnp.where(inside, turned[n], turned[n + 1])
        sums[3] = sums[3] + jnp.where(inside, turned[3], 0.0)
        wrapped = wrapped + jnp.where(inside, 0.0, turned[0])
    wrapped = jnp.where(row_index((8, LANES)) == 7, 0.0, pltpu.roll(wrapped, 7, 0))
    sums[3] = sums[3] + wrapped
    for h in range(4):
        dwide_ref[pl.ds(OWN * h + c, 8, stride=32), :] = sums[h] * (1.0 / SEQ)


def widen(ref, wide_ref):
    for v in range(2):
        wide_ref[v] = ref[:, :, v * LANES : (v + 1) * LANES].astype(F32).reshape(256, LANES)


def kernel(
    n_ctx, n_dp, n_y,
    up_ref, gate_ref, in_ref, filt_ref, gain_ref,
    yrecv, drecv,
    up, gate, raw, filt, gain, wide, gsend, xsend, hsend, hpass, grecv, xrecv, hrecv, gwide, xwide, hwide, toep, win, wint,
    yall, ywide, ysend, xall, xs, sums, dwide, dsend,
    hello, hello_z, load_sem,
    h_send_sem, h_recv_sem, t_send_sem, t_recv_sem, g_send_sem, g_recv_sem, x_send_sem, x_recv_sem,
    y_send_sem, y_recv_sem, d_send_sem, d_recv_sem,
):
    me_ctx = lax.axis_index("ctx")
    me_dp = lax.axis_index("dp")
    half = n_ctx // 2
    me_hi = me_ctx // half
    me_lo = lax.rem(me_ctx, half)
    n_z = n_dp // n_y
    me_z = me_dp // n_y
    me_y = lax.rem(me_dp, n_y)

    def far_ctx(step):
        peer = (1 - me_hi) * half + lax.rem(me_lo + step, half)
        return peer, {"ctx": peer, "dp": me_dp}

    def near_ctx(step):
        peer = me_hi * half + lax.rem(me_lo + step, half)
        return peer, {"ctx": peer, "dp": me_dp}

    def over_dp(step):
        peer = lax.rem(me_dp + step, n_dp)
        return peer, {"ctx": me_ctx, "dp": peer}

    def to_dp(peer):
        return peer, {"ctx": me_ctx, "dp": peer}

    def over_y(step):
        peer = lax.rem(me_y + step, n_y)
        return peer, {"ctx": me_ctx, "dp": me_z * n_y + peer}

    def over_z(step):
        peer = lax.rem(me_z + step, n_z)
        return peer, {"ctx": me_ctx, "dp": peer * n_y + me_y}

    def pieces(src, dst, sem, count):
        size = dst.shape[0] // count
        return [
            pltpu.make_async_copy(src.at[pl.ds(n * size, size)], dst.at[pl.ds(n * size, size)], sem)
            for n in range(count)
        ]

    def load(n, src, dst, count=4):
        for piece in pieces(src, dst, load_sem.at[n], count):
            piece.start()

    def loaded(n, dst):
        pltpu.make_async_copy(dst, dst, load_sem.at[n]).wait()

    load(0, up_ref, up)
    load(1, gate_ref, gate)
    barrier = pltpu.get_barrier_semaphore()

    def greet(first, last, over):
        @pl.loop(first, last)
        def _(step):
            pl.semaphore_signal(barrier, inc=1, device_id=over(step)[1], device_id_type=MESH)

    greet(0, half, far_ctx)
    def edge(y):
        return jnp.minimum(y, n_y - y)

    def sooner(step):
        return edge(lax.rem(me_y + step, n_y)) < edge(me_y)

    @pl.when(me_hi == 0)
    def _():
        greet(1, n_dp, over_dp)

    @pl.when(me_hi == 1)
    def _():
        greet(1, 3, over_y)
        greet(n_y - 2, n_y, over_y)
        for step in range(3, n_y - 2):
            peer, where = over_y(step)

            @pl.when(edge(me_y) < edge(peer))
            def _():
                pl.semaphore_signal(barrier, inc=1, device_id=where, device_id_type=MESH)

        for z in range(n_z):
            where = {"ctx": me_ctx, "dp": z * n_y + me_y}

            @pl.when(jnp.logical_and(z >= me_z - 1, z != me_z))
            def _():
                pl.semaphore_signal(barrier, inc=1, device_id=where, device_id_type=MESH)

    heard = 4 + me_z + jnp.where(me_z < n_z - 1, 1, 0)
    for step in range(3, n_y - 2):
        heard = heard + jnp.where(sooner(step), 1, 0)
    greeted = n_ctx - 1 + jnp.where(me_hi == 1, heard, n_dp - 1)

    greet(1, half, near_ctx)

    def scatter(first, last, over, me, src, dst, send_sem, recv_sem):
        @pl.loop(first, last)
        def _(step):
            peer, where = over(step)
            pltpu.make_async_remote_copy(
                src_ref=src.at[peer], dst_ref=dst.at[me], send_sem=send_sem, recv_sem=recv_sem,
                device_id=where, device_id_type=MESH,
            ).start()

    def keep_own(me, src, dst, recv_sem):
        pltpu.make_async_copy(src.at[me], dst.at[me], recv_sem).start()

    def pass_on(origin, src):
        pltpu.make_async_copy(src.at[origin, me_z], hrecv.at[me_z, origin], t_recv_sem).start()

        @pl.loop(1, n_z)
        def _(step):
            peer, where = over_z(step)
            pltpu.make_async_remote_copy(
                src_ref=src.at[origin, peer], dst_ref=hrecv.at[me_z, origin], send_sem=t_send_sem,
                recv_sem=t_recv_sem, device_id=where, device_id_type=MESH,
            ).start()

    def arrive(dst, sem):
        pltpu.make_async_copy(dst, dst, sem).wait()

    def sent(count, src, sem):
        part = src.at[pl.ds(0, count - 1)]
        pltpu.make_async_copy(part, part, sem).wait()

    load(2, in_ref, raw)
    load(3, filt_ref, filt)
    load(4, gain_ref, gain, 1)
    loaded(0, up)
    loaded(1, gate)
    wide[...] = (up[...].astype(F32) * gate[...].astype(F32)).astype(BF16).astype(F32)
    spread_rows(wide, gsend)
    pl.semaphore_wait(barrier, greeted)
    scatter(0, half, far_ctx, me_ctx, gsend, grecv, g_send_sem, g_recv_sem)
    @pl.when(me_hi == 1)
    def _():
        for step in (2, n_y - 2):
            pl.semaphore_signal(hello, inc=1, device_id=over_y(step)[1], device_id_type=MESH)
        for z in range(n_z - 2):

            @pl.when(z < me_z - 1)
            def _():
                pl.semaphore_signal(
                    hello_z, inc=1, device_id={"ctx": me_ctx, "dp": z * n_y + me_y}, device_id_type=MESH
                )

    loaded(3, filt)
    for z in range(n_z):
        hsend[:, z] = filt[z * n_y : (z + 1) * n_y].astype(BF16)
    @pl.when(me_hi == 0)
    def _():
        pltpu.make_async_copy(hsend.at[me_y, me_z], hrecv.at[me_z, me_y], t_recv_sem).start()

        @pl.loop(1, n_dp)
        def _(step):
            peer, where = over_dp(step)
            pltpu.make_async_remote_copy(
                src_ref=hsend.at[lax.rem(peer, n_y), peer // n_y], dst_ref=hrecv.at[me_z, me_y],
                send_sem=t_send_sem, recv_sem=t_recv_sem, device_id=where, device_id_type=MESH,
            ).start()

    @pl.when(me_hi == 1)
    def _():
        scatter(1, 3, over_y, me_y, hsend, hpass, h_send_sem, h_recv_sem.at[0])
        scatter(n_y - 2, n_y, over_y, me_y, hsend, hpass, h_send_sem, h_recv_sem.at[0])
        for step in range(3, n_y - 2):

            @pl.when(sooner(step))
            def _():
                scatter(step, step + 1, over_y, me_y, hsend, hpass, h_send_sem, h_recv_sem.at[1])

    loaded(2, raw)
    wide[...] = raw[...].astype(F32)
    spread_rows(wide, xsend)

    @pl.when(me_hi == 1)
    def _():
        scatter(0, half, far_ctx, me_ctx, xsend, xrecv, x_send_sem, x_recv_sem)

    scatter(1, half, near_ctx, me_ctx, gsend, grecv, g_send_sem, g_recv_sem)
    scatter(1, half, near_ctx, me_ctx, xsend, xrecv, x_send_sem, x_recv_sem)
    keep_own(me_ctx, gsend, grecv, g_recv_sem)
    keep_own(me_ctx, xsend, xrecv, x_recv_sem)
    loaded(4, gain)
    @pl.when(me_hi == 1)
    def _():
        pl.semaphore_wait(hello, 2)
        for step in range(3, n_y - 2):

            @pl.when(jnp.logical_not(sooner(step)))
            def _():
                scatter(step, step + 1, over_y, me_y, hsend, hpass, h_send_sem, h_recv_sem.at[1])


        for z in range(n_z - 2):

            @pl.when(z == me_z)
            def _():
                pl.semaphore_wait(hello_z, n_z - 2 - z)

        pass_on(me_y, hsend)
        arrive(hpass.at[pl.ds(0, 4)], h_recv_sem.at[0])
        for step in (1, n_y - 1, 2, n_y - 2):
            pass_on(lax.rem(me_y + step, n_y), hpass)
        arrive(hpass.at[pl.ds(0, n_y - 5)], h_recv_sem.at[1])
        for step in range(3, n_y - 2):
            pass_on(lax.rem(me_y + step, n_y), hpass)

    arrive(grecv, g_recv_sem)

    @pl.when(me_hi == 0)
    def _():
        scatter(0, half, far_ctx, me_ctx, xsend, xrecv, x_send_sem, x_recv_sem)

    widen(grecv, gwide)
    for c in range(OWN):
        build_windows(gwide, win, c)
    for c in range(OWN):
        wint[c] = win[c].T

    @pl.loop(0, 2)
    def _(turn):
        @pl.when(turn != me_hi)
        def _():
            arrive(hrecv, t_recv_sem)
            hwide[...] = hrecv[...].astype(F32).reshape(n_dp * OWN, LANES)
            for c in range(OWN):
                build_toeplitz(hwide, toep, c)

            for h in range(2):
                for c in range(OWN):
                    back_rows(toep, wint, yall, c, h)
                finish_back(yall, gwide, gain, me_ctx * OWN, ywide.at[h], ysend, h)

                @pl.loop(0, n_ctx // 2)
                def _(step):
                    block = half // 2 * (step // (half // 2)) + lax.rem(me_lo // 2 + step, half // 2)
                    peer = 2 * block + h

                    @pl.when(peer != me_ctx)
                    def _():
                        pltpu.make_async_remote_copy(
                            src_ref=ysend.at[block, h], dst_ref=yrecv.at[me_ctx], send_sem=y_send_sem,
                            recv_sem=y_recv_sem, device_id={"ctx": peer, "dp": me_dp}, device_id_type=MESH,
                        ).start()

                    @pl.when(peer == me_ctx)
                    def _():
                        pltpu.make_async_copy(ysend.at[block, h], yrecv.at[me_ctx], y_recv_sem).start()

        @pl.when(turn == me_hi)
        def _():
            arrive(xrecv, x_recv_sem)
            widen(xrecv, xwide)
            turn_inputs(xwide, xall)
            for c in range(OWN):
                shift_inputs(xall, xs, c)
            for c in range(OWN):
                filter_rows(xs, win, sums, dwide, c)
            dsend[...] = dwide[...].reshape(n_dp, OWN, LANES).astype(BF16)
            scatter(0, me_dp, to_dp, me_dp, dsend, drecv, d_send_sem, d_recv_sem)
            scatter(me_dp + 1, n_dp, to_dp, me_dp, dsend, drecv, d_send_sem, d_recv_sem)
            keep_own(me_dp, dsend, drecv, d_recv_sem)

    @pl.when(me_hi == 0)
    def _():
        sent(n_dp, hrecv.reshape(n_dp, OWN, LANES), t_send_sem)

    @pl.when(me_hi == 1)
    def _():
        sent(n_y, hsend, h_send_sem)
        sent(n_z, hrecv, t_send_sem)

    sent(n_ctx, gsend, g_send_sem)
    sent(n_ctx, xsend, x_send_sem)
    sent(n_ctx, yrecv, y_send_sem)
    sent(n_dp, dsend, d_send_sem)
    arrive(yrecv, y_recv_sem)
    arrive(drecv, d_recv_sem)


def finish_kernel(y_in, d_in, out_ref, grad_ref, wide, out, grad, store_sem):
    def store(n, src, dst, first, size):
        part = pl.ds(first, size)
        pltpu.make_async_copy(src.at[part], dst.at[part], store_sem.at[n]).start()

    for n in range(4):
        grad[8 * n : 8 * n + 8] = d_in[8 * n : 8 * n + 8].astype(F32)
        store(0, grad, grad_ref, 8 * n, 8)
    for n in range(2):
        time = slice(n * LANES, (n + 1) * LANES)
        back = y_in[:, :, time].astype(F32)
        for s in range(SEQ):
            wide[pl.ds(256 * n + s, LANES, stride=2), :] = (
                back[:, s * OWN : (s + 1) * OWN, :].reshape(16 * OWN, LANES).T
            )
        out[256 * n : 256 * n + 256] = wide[256 * n : 256 * n + 256].astype(BF16)
        for k in range(2):
            store(1, out, out_ref, 256 * n + 128 * k, 128)
    pltpu.make_async_copy(grad, grad_ref, store_sem.at[0]).wait()
    pltpu.make_async_copy(out, out_ref, store_sem.at[1]).wait()


def body(upstream, gate_value, conv_input, filters, skip_gain):
    n_ctx = lax.axis_size("ctx")
    n_dp = lax.axis_size("dp")
    n_y = LINE
    n_z = n_dp // n_y
    rows = upstream.shape[0] * upstream.shape[1]
    width = upstream.shape[2]
    block = (16, 16, 256)
    hbm = pl.BlockSpec(memory_space=pltpu.HBM)
    grant = 56 * 1024 * 1024
    back, grads = pl.pallas_call(
        functools.partial(kernel, n_ctx, n_dp, n_y),
        out_shape=(pltpu.VMEM(block, BF16), pltpu.VMEM(filters.shape, BF16)),
        in_specs=[hbm] * 5,
        out_specs=[pl.BlockSpec(memory_space=pltpu.VMEM)] * 2,
        scratch_shapes=[
            pltpu.VMEM((rows, width), BF16),
            pltpu.VMEM((rows, width), BF16),
            pltpu.VMEM((rows, width), BF16),
            pltpu.VMEM(filters.shape, F32),
            pltpu.SMEM(skip_gain.shape, F32),
            pltpu.VMEM((rows, width), F32),
            pltpu.VMEM(block, BF16),
            pltpu.VMEM(block, BF16),
            pltpu.VMEM((n_y, n_z, OWN, LANES), BF16),
            pltpu.VMEM((n_y, n_z, OWN, LANES), BF16),
            pltpu.VMEM(block, BF16),
            pltpu.VMEM(block, BF16),
            pltpu.VMEM((n_z, n_y, OWN, LANES), BF16),
            pltpu.VMEM((2, 256, LANES), F32),
            pltpu.VMEM((2, 256, LANES), F32),
            pltpu.VMEM((n_dp * OWN, LANES), F32),
            pltpu.VMEM((OWN, 8 * HOP, SPAN), BF16),
            pltpu.VMEM((OWN, SPAN, SPAN), BF16),
            pltpu.VMEM((OWN, SPAN, SPAN), BF16),
            pltpu.VMEM((OWN * HOP, SPAN), F32),
            pltpu.VMEM((2, 2, 128, LANES), F32),
            pltpu.VMEM((8, 2, 16, 256), BF16),
            pltpu.VMEM((OWN * HOP, SPAN), F32),
            pltpu.VMEM((OWN, 8 * HOP, SPAN), BF16),
            pltpu.VMEM((OWN, 4, 8 * HOP, LANES), F32),
            pltpu.VMEM((n_dp * OWN, LANES), F32),
            pltpu.VMEM(filters.shape, BF16),
        ]
        + [pltpu.SemaphoreType.REGULAR] * 2
        + [pltpu.SemaphoreType.DMA((5,))]
        + [pltpu.SemaphoreType.DMA, pltpu.SemaphoreType.DMA((2,))]
        + [pltpu.SemaphoreType.DMA] * 10,
        compiler_params=pltpu.CompilerParams(collective_id=0, has_side_effects=True, vmem_limit_bytes=grant),
    )(
        upstream.reshape(rows, width),
        gate_value.reshape(rows, width),
        conv_input.reshape(rows, width),
        filters,
        skip_gain,
    )
    out, grad = pl.pallas_call(
        finish_kernel,
        out_shape=(jax.ShapeDtypeStruct((rows, width), BF16), jax.ShapeDtypeStruct(filters.shape, F32)),
        in_specs=[pl.BlockSpec(memory_space=pltpu.VMEM)] * 2,
        out_specs=[hbm] * 2,
        scratch_shapes=[
            pltpu.VMEM((rows, width), F32),
            pltpu.VMEM((rows, width), BF16),
            pltpu.VMEM(filters.shape, F32),
            pltpu.SemaphoreType.DMA((2,)),
        ],
        compiler_params=pltpu.CompilerParams(vmem_limit_bytes=16 * 1024 * 1024),
    )(back, grads)
    return out.reshape(upstream.shape), grad


def solution(mesh):
    in_specs = (
        P("ctx", None, "dp"),
        P("ctx", None, "dp"),
        P("ctx", None, "dp"),
        P(None, "ctx", "dp"),
        P("dp"),
    )
    out_specs = (P("ctx", None, "dp"), P(None, "ctx", "dp"))
    return jax.shard_map(body, mesh=mesh, in_specs=in_specs, out_specs=out_specs, check_vma=False)
```

```python
import functools

import jax
import jax.numpy as jnp
from jax import lax
from jax.experimental import pallas as pl
from jax.experimental.pallas import tpu as pltpu
from jax.sharding import PartitionSpec as P

MESH = pl.DeviceIdType.MESH
F32 = jnp.float32
BF16 = jnp.bfloat16

SPAN = 512
HOP = 16
LANES = 128
OWN = 8
SEQ = 2
FIRST = 1
LINE = 8


def lane_index(shape):
    return lax.broadcasted_iota(jnp.int32, shape, len(shape) - 1)


def row_index(shape):
    return lax.broadcasted_iota(jnp.int32, shape, len(shape) - 2)


def swap_groups(blocks):
    blocks = list(blocks)
    lane = lane_index((HOP, LANES)) // HOP
    for bit in (1, 2, 4):
        upper = (lane & bit) != 0
        for r in range(8):
            if r & bit:
                continue
            low, high = blocks[r], blocks[r | bit]
            blocks[r] = jnp.where(upper, pltpu.roll(high, HOP * bit, 1), low)
            blocks[r | bit] = jnp.where(upper, high, pltpu.roll(low, LANES - HOP * bit, 1))
    return blocks


def spread_rows(wide_ref, send_ref):
    halves = []
    for s in range(SEQ):
        part = wide_ref[pl.ds(s, 256, stride=2), :]
        halves.append(part.T.reshape(16, OWN, 256))
    send_ref[...] = jnp.concatenate(halves, axis=1).astype(BF16)


def build_toeplitz(hwide_ref, toep_ref, c):
    tiles = [hwide_ref[pl.ds(OWN * h + c, 8, stride=32), :] for h in range(4)]
    before = jnp.where(row_index((8, LANES)) == 0, 0.0, pltpu.roll(tiles[3], 1, 0))
    tiles = [before] + tiles
    keep = lane_index((HOP, LANES)) >= row_index((HOP, LANES))
    for q in range(8):
        turned = [
            pltpu.roll(jnp.broadcast_to(tile[q : q + 1, :], (HOP, LANES)), 0, 1, stride=1, stride_axis=0)
            for tile in tiles
        ]
        rows = [jnp.where(keep, turned[h + 1], turned[h]) for h in range(4)]
        toep_ref[c, q * HOP : (q + 1) * HOP, :] = jnp.concatenate(rows, axis=1).astype(BF16)


def own_rows(wide_ref, c):
    seqs = []
    for s in range(SEQ):
        seqs.append(
            jnp.concatenate(
                [
                    wide_ref[v, pl.ds(h * 16 + s * OWN + c, 8, stride=32), :]
                    for h in range(2)
                    for v in range(2)
                ],
                axis=1,
            )
        )
    return jnp.concatenate(seqs, axis=0)


def build_windows(gwide_ref, win_ref, c):
    here = own_rows(gwide_ref, c)
    after = pltpu.roll(here, 15, 0)
    after = jnp.where(row_index((16, SPAN)) % 8 == 7, 0.0, after)
    both = jnp.concatenate([here, after], axis=1)
    for r in range(8):
        turned = both if r == 0 else pltpu.roll(both, 2 * SPAN - HOP * r, 1)
        for jt in range(4):
            j = 8 * jt + r
            win_ref[c, j * 16 : (j + 1) * 16, :] = turned[:, LANES * jt : LANES * jt + SPAN].astype(BF16)


def back_rows(toep_ref, wint_ref, yall_ref, c, h):
    out = jnp.dot(toep_ref[c], wint_ref[c, :, 256 * h : 256 * h + 256], preferred_element_type=F32)
    group = lane_index((HOP, LANES)) % 8
    for n in range(2):
        tile = out[:, n * LANES : (n + 1) * LANES]
        total = tile[0:HOP]
        for q in range(1, 8):
            turned = pltpu.roll(tile[q * HOP : (q + 1) * HOP], LANES - q, 1)
            total = total + jnp.where(group < 8 - q, turned, 0.0)
        yall_ref[c * HOP : (c + 1) * HOP, 256 * h + n * LANES : 256 * h + (n + 1) * LANES] = total


def finish_back(yall_ref, gwide_ref, gain_ref, first_gain, ywide_ref, ysend_ref, h):
    cols = []
    for n in (2 * h, 2 * h + 1):
        turned = yall_ref[:, n * LANES : (n + 1) * LANES].T
        cols.append(swap_groups([turned[HOP * r : HOP * (r + 1)] for r in range(8)]))
    for c in range(OWN):
        gain = gain_ref[first_gain + c]
        for v in range(2):
            for s in range(SEQ):
                rows = cols[v][c][8 * s : 8 * s + 8]
                here = gwide_ref[v, pl.ds(h * 16 + s * OWN + c, 8, stride=32), :]
                ywide_ref[v, pl.ds(s * OWN + c, 8, stride=16), :] = rows + gain * here
    for v in range(2):
        ysend_ref[:, h, :, v * LANES : (v + 1) * LANES] = ywide_ref[v].reshape(8, 16, LANES).astype(BF16)


def turn_inputs(xwide_ref, xall_ref):
    rows = [own_rows(xwide_ref, c) for c in range(OWN)]
    for n in range(4):
        blocks = swap_groups([row[:, n * LANES : (n + 1) * LANES] for row in rows])
        xall_ref[:, n * LANES : (n + 1) * LANES] = jnp.concatenate(blocks, axis=0).T


def shift_inputs(xall_ref, xs_ref, c):
    group = lane_index((HOP, LANES)) % 8
    for n in range(4):
        tile = xall_ref[c * HOP : (c + 1) * HOP, n * LANES : (n + 1) * LANES].astype(BF16)
        for q in range(8):
            turned = tile if q == 0 else jnp.where(group >= q, pltpu.roll(tile, q, 1), jnp.zeros_like(tile))
            xs_ref[c, q * HOP : (q + 1) * HOP, n * LANES : (n + 1) * LANES] = turned


def filter_rows(xs_ref, win_ref, sums_ref, dwide_ref, c):
    out = jnp.dot(xs_ref[c], win_ref[c], preferred_element_type=F32)
    for n in range(4):
        sums_ref[c, n] = out[:, n * LANES : (n + 1) * LANES]
    lane = lane_index((8, LANES))
    rows = [[sums_ref[c, n, pl.ds(a, 8, stride=HOP), :] for n in range(4)] for a in range(HOP)]
    sums = rows[0]
    wrapped = jnp.zeros((8, LANES), F32)
    for a in range(1, HOP):
        turned = [pltpu.roll(row, LANES - a, 1) for row in rows[a]]
        inside = lane < LANES - a
        for n in range(3):
            sums[n] = sums[n] + jnp.where(inside, turned[n], turned[n + 1])
        sums[3] = sums[3] + jnp.where(inside, turned[3], 0.0)
        wrapped = wrapped + jnp.where(inside, 0.0, turned[0])
    wrapped = jnp.where(row_index((8, LANES)) == 7, 0.0, pltpu.roll(wrapped, 7, 0))
    sums[3] = sums[3] + wrapped
    for h in range(4):
        dwide_ref[pl.ds(OWN * h + c, 8, stride=32), :] = sums[h] * (1.0 / SEQ)


def widen(ref, wide_ref):
    for v in range(2):
        wide_ref[v] = ref[:, :, v * LANES : (v + 1) * LANES].astype(F32).reshape(256, LANES)


def kernel(
    n_ctx, n_dp, n_y,
    up_ref, gate_ref, in_ref, filt_ref, gain_ref,
    yrecv, drecv,
    up, gate, raw, filt, gain, wide, gsend, xsend, hsend, hpass, grecv, xrecv, hrecv, gwide, xwide, hwide, toep, win, wint,
    yall, ywide, ysend, xall, xs, sums, dwide, dsend,
    hello, hello_z, load_sem,
    h_send_sem, h_recv_sem, t_send_sem, t_recv_sem, g_send_sem, g_recv_sem, x_send_sem, x_recv_sem,
    y_send_sem, y_recv_sem, d_send_sem, d_recv_sem,
):
    me_ctx = lax.axis_index("ctx")
    me_dp = lax.axis_index("dp")
    half = n_ctx // 2
    me_hi = me_ctx // half
    me_lo = lax.rem(me_ctx, half)
    n_z = n_dp // n_y
    me_z = me_dp // n_y
    me_y = lax.rem(me_dp, n_y)

    def far_ctx(step):
        peer = (1 - me_hi) * half + lax.rem(me_lo + step, half)
        return peer, {"ctx": peer, "dp": me_dp}

    def first_far(step):
        peer = (1 - me_hi) * half + FIRST
        return peer, {"ctx": peer, "dp": me_dp}

    def other_far(step):
        peer = (1 - me_hi) * half + lax.rem(FIRST + 1 + lax.rem(me_lo + step, half - 1), half)
        return peer, {"ctx": peer, "dp": me_dp}

    def near_ctx(step):
        peer = me_hi * half + lax.rem(me_lo + step, half)
        return peer, {"ctx": peer, "dp": me_dp}

    def over_dp(step):
        peer = lax.rem(me_dp + step, n_dp)
        return peer, {"ctx": me_ctx, "dp": peer}

    def to_dp(peer):
        return peer, {"ctx": me_ctx, "dp": peer}

    def over_y(step):
        peer = lax.rem(me_y + step, n_y)
        return peer, {"ctx": me_ctx, "dp": me_z * n_y + peer}

    def over_z(step):
        peer = lax.rem(me_z + step, n_z)
        return peer, {"ctx": me_ctx, "dp": peer * n_y + me_y}

    def pieces(src, dst, sem, count):
        size = dst.shape[0] // count
        return [
            pltpu.make_async_copy(src.at[pl.ds(n * size, size)], dst.at[pl.ds(n * size, size)], sem)
            for n in range(count)
        ]

    def load(n, src, dst, count=4):
        for piece in pieces(src, dst, load_sem.at[n], count):
            piece.start()

    def loaded(n, dst):
        pltpu.make_async_copy(dst, dst, load_sem.at[n]).wait()

    load(0, up_ref, up)
    load(1, gate_ref, gate)
    barrier = pltpu.get_barrier_semaphore()

    def greet(first, last, over):
        @pl.loop(first, last)
        def _(step):
            pl.semaphore_signal(barrier, inc=1, device_id=over(step)[1], device_id_type=MESH)

    greet(0, half, far_ctx)
    def edge(y):
        return jnp.minimum(y, n_y - y)

    def sooner(step):
        return edge(lax.rem(me_y + step, n_y)) < edge(me_y)

    @pl.when(me_hi == 0)
    def _():
        greet(1, n_dp, over_dp)

    @pl.when(me_hi == 1)
    def _():
        greet(1, 3, over_y)
        greet(n_y - 2, n_y, over_y)
        for step in range(3, n_y - 2):
            peer, where = over_y(step)

            @pl.when(edge(me_y) < edge(peer))
            def _():
                pl.semaphore_signal(barrier, inc=1, device_id=where, device_id_type=MESH)

        for z in range(n_z):
            where = {"ctx": me_ctx, "dp": z * n_y + me_y}

            @pl.when(jnp.logical_and(z >= me_z - 1, z != me_z))
            def _():
                pl.semaphore_signal(barrier, inc=1, device_id=where, device_id_type=MESH)

    heard = 4 + me_z + jnp.where(me_z < n_z - 1, 1, 0)
    for step in range(3, n_y - 2):
        heard = heard + jnp.where(sooner(step), 1, 0)
    greeted = n_ctx - 1 + jnp.where(me_hi == 1, heard, n_dp - 1)

    greet(1, half, near_ctx)

    def scatter(first, last, over, me, src, dst, send_sem, recv_sem):
        @pl.loop(first, last)
        def _(step):
            peer, where = over(step)
            pltpu.make_async_remote_copy(
                src_ref=src.at[peer], dst_ref=dst.at[me], send_sem=send_sem, recv_sem=recv_sem,
                device_id=where, device_id_type=MESH,
            ).start()

    def keep_own(me, src, dst, recv_sem):
        pltpu.make_async_copy(src.at[me], dst.at[me], recv_sem).start()

    def pass_on(origin, src):
        pltpu.make_async_copy(src.at[origin, me_z], hrecv.at[me_z, origin], t_recv_sem).start()

        @pl.loop(1, n_z)
        def _(step):
            peer, where = over_z(step)
            pltpu.make_async_remote_copy(
                src_ref=src.at[origin, peer], dst_ref=hrecv.at[me_z, origin], send_sem=t_send_sem,
                recv_sem=t_recv_sem, device_id=where, device_id_type=MESH,
            ).start()

    def arrive(dst, sem):
        pltpu.make_async_copy(dst, dst, sem).wait()

    def sent(count, src, sem):
        part = src.at[pl.ds(0, count - 1)]
        pltpu.make_async_copy(part, part, sem).wait()

    load(2, in_ref, raw)
    load(3, filt_ref, filt)
    load(4, gain_ref, gain, 1)
    loaded(0, up)
    loaded(1, gate)
    wide[...] = (up[...].astype(F32) * gate[...].astype(F32)).astype(BF16).astype(F32)
    spread_rows(wide, gsend)
    loaded(2, raw)
    wide[...] = raw[...].astype(F32)
    spread_rows(wide, xsend)
    pl.semaphore_wait(barrier, greeted)
    scatter(0, 1, first_far, me_ctx, gsend, grecv, g_send_sem, g_recv_sem)

    @pl.when(me_hi == 1)
    def _():
        scatter(0, 1, first_far, me_ctx, xsend, xrecv, x_send_sem, x_recv_sem)

    scatter(0, half - 1, other_far, me_ctx, gsend, grecv, g_send_sem, g_recv_sem)
    @pl.when(me_hi == 1)
    def _():
        for step in (2, n_y - 2):
            pl.semaphore_signal(hello, inc=1, device_id=over_y(step)[1], device_id_type=MESH)
        for z in range(n_z - 2):

            @pl.when(z < me_z - 1)
            def _():
                pl.semaphore_signal(
                    hello_z, inc=1, device_id={"ctx": me_ctx, "dp": z * n_y + me_y}, device_id_type=MESH
                )

    loaded(3, filt)
    for z in range(n_z):
        hsend[:, z] = filt[z * n_y : (z + 1) * n_y].astype(BF16)
    @pl.when(me_hi == 0)
    def _():
        pltpu.make_async_copy(hsend.at[me_y, me_z], hrecv.at[me_z, me_y], t_recv_sem).start()

        @pl.loop(1, n_dp)
        def _(step):
            peer, where = over_dp(step)
            pltpu.make_async_remote_copy(
                src_ref=hsend.at[lax.rem(peer, n_y), peer // n_y], dst_ref=hrecv.at[me_z, me_y],
                send_sem=t_send_sem, recv_sem=t_recv_sem, device_id=where, device_id_type=MESH,
            ).start()

    @pl.when(me_hi == 1)
    def _():
        scatter(1, 3, over_y, me_y, hsend, hpass, h_send_sem, h_recv_sem.at[0])
        scatter(n_y - 2, n_y, over_y, me_y, hsend, hpass, h_send_sem, h_recv_sem.at[0])
        for step in range(3, n_y - 2):

            @pl.when(sooner(step))
            def _():
                scatter(step, step + 1, over_y, me_y, hsend, hpass, h_send_sem, h_recv_sem.at[1])


    @pl.when(me_hi == 1)
    def _():
        scatter(0, half - 1, other_far, me_ctx, xsend, xrecv, x_send_sem, x_recv_sem)

    scatter(1, half, near_ctx, me_ctx, gsend, grecv, g_send_sem, g_recv_sem)
    scatter(1, half, near_ctx, me_ctx, xsend, xrecv, x_send_sem, x_recv_sem)
    keep_own(me_ctx, gsend, grecv, g_recv_sem)
    keep_own(me_ctx, xsend, xrecv, x_recv_sem)
    loaded(4, gain)
    @pl.when(me_hi == 1)
    def _():
        pl.semaphore_wait(hello, 2)
        for step in range(3, n_y - 2):

            @pl.when(jnp.logical_not(sooner(step)))
            def _():
                scatter(step, step + 1, over_y, me_y, hsend, hpass, h_send_sem, h_recv_sem.at[1])


        for z in range(n_z - 2):

            @pl.when(z == me_z)
            def _():
                pl.semaphore_wait(hello_z, n_z - 2 - z)

        pass_on(me_y, hsend)
        arrive(hpass.at[pl.ds(0, 4)], h_recv_sem.at[0])
        for step in (1, n_y - 1, 2, n_y - 2):
            pass_on(lax.rem(me_y + step, n_y), hpass)
        arrive(hpass.at[pl.ds(0, n_y - 5)], h_recv_sem.at[1])
        for step in range(3, n_y - 2):
            pass_on(lax.rem(me_y + step, n_y), hpass)

    arrive(grecv, g_recv_sem)

    @pl.when(me_hi == 0)
    def _():
        scatter(0, half, far_ctx, me_ctx, xsend, xrecv, x_send_sem, x_recv_sem)

    widen(grecv, gwide)
    for c in range(OWN):
        build_windows(gwide, win, c)
    for c in range(OWN):
        wint[c] = win[c].T

    @pl.loop(0, 2)
    def _(turn):
        @pl.when(turn != me_hi)
        def _():
            arrive(hrecv, t_recv_sem)
            hwide[...] = hrecv[...].astype(F32).reshape(n_dp * OWN, LANES)
            for c in range(OWN):
                build_toeplitz(hwide, toep, c)

            for h in range(2):
                for c in range(OWN):
                    back_rows(toep, wint, yall, c, h)
                finish_back(yall, gwide, gain, me_ctx * OWN, ywide.at[h], ysend, h)

                @pl.loop(0, n_ctx // 2)
                def _(step):
                    block = half // 2 * (step // (half // 2)) + lax.rem(me_lo // 2 + step, half // 2)
                    peer = 2 * block + h

                    @pl.when(peer != me_ctx)
                    def _():
                        pltpu.make_async_remote_copy(
                            src_ref=ysend.at[block, h], dst_ref=yrecv.at[me_ctx], send_sem=y_send_sem,
                            recv_sem=y_recv_sem, device_id={"ctx": peer, "dp": me_dp}, device_id_type=MESH,
                        ).start()

                    @pl.when(peer == me_ctx)
                    def _():
                        pltpu.make_async_copy(ysend.at[block, h], yrecv.at[me_ctx], y_recv_sem).start()

        @pl.when(turn == me_hi)
        def _():
            arrive(xrecv, x_recv_sem)
            widen(xrecv, xwide)
            turn_inputs(xwide, xall)
            for c in range(OWN):
                shift_inputs(xall, xs, c)
            for c in range(OWN):
                filter_rows(xs, win, sums, dwide, c)
            dsend[...] = dwide[...].reshape(n_dp, OWN, LANES).astype(BF16)
            scatter(0, me_dp, to_dp, me_dp, dsend, drecv, d_send_sem, d_recv_sem)
            scatter(me_dp + 1, n_dp, to_dp, me_dp, dsend, drecv, d_send_sem, d_recv_sem)
            keep_own(me_dp, dsend, drecv, d_recv_sem)

    @pl.when(me_hi == 0)
    def _():
        sent(n_dp, hrecv.reshape(n_dp, OWN, LANES), t_send_sem)

    @pl.when(me_hi == 1)
    def _():
        sent(n_y, hsend, h_send_sem)
        sent(n_z, hrecv, t_send_sem)

    sent(n_ctx, gsend, g_send_sem)
    sent(n_ctx, xsend, x_send_sem)
    sent(n_ctx, yrecv, y_send_sem)
    sent(n_dp, dsend, d_send_sem)
    arrive(yrecv, y_recv_sem)
    arrive(drecv, d_recv_sem)


def finish_kernel(y_in, d_in, out_ref, grad_ref, wide, out, grad, store_sem):
    def store(n, src, dst, first, size):
        part = pl.ds(first, size)
        pltpu.make_async_copy(src.at[part], dst.at[part], store_sem.at[n]).start()

    for n in range(4):
        grad[8 * n : 8 * n + 8] = d_in[8 * n : 8 * n + 8].astype(F32)
        store(0, grad, grad_ref, 8 * n, 8)
    for n in range(2):
        time = slice(n * LANES, (n + 1) * LANES)
        back = y_in[:, :, time].astype(F32)
        for s in range(SEQ):
            wide[pl.ds(256 * n + s, LANES, stride=2), :] = (
                back[:, s * OWN : (s + 1) * OWN, :].reshape(16 * OWN, LANES).T
            )
        out[256 * n : 256 * n + 256] = wide[256 * n : 256 * n + 256].astype(BF16)
        for k in range(2):
            store(1, out, out_ref, 256 * n + 128 * k, 128)
    pltpu.make_async_copy(grad, grad_ref, store_sem.at[0]).wait()
    pltpu.make_async_copy(out, out_ref, store_sem.at[1]).wait()


def body(upstream, gate_value, conv_input, filters, skip_gain):
    n_ctx = lax.axis_size("ctx")
    n_dp = lax.axis_size("dp")
    n_y = LINE
    n_z = n_dp // n_y
    rows = upstream.shape[0] * upstream.shape[1]
    width = upstream.shape[2]
    block = (16, 16, 256)
    hbm = pl.BlockSpec(memory_space=pltpu.HBM)
    grant = 56 * 1024 * 1024
    back, grads = pl.pallas_call(
        functools.partial(kernel, n_ctx, n_dp, n_y),
        out_shape=(pltpu.VMEM(block, BF16), pltpu.VMEM(filters.shape, BF16)),
        in_specs=[hbm] * 5,
        out_specs=[pl.BlockSpec(memory_space=pltpu.VMEM)] * 2,
        scratch_shapes=[
            pltpu.VMEM((rows, width), BF16),
            pltpu.VMEM((rows, width), BF16),
            pltpu.VMEM((rows, width), BF16),
            pltpu.VMEM(filters.shape, F32),
            pltpu.SMEM(skip_gain.shape, F32),
            pltpu.VMEM((rows, width), F32),
            pltpu.VMEM(block, BF16),
            pltpu.VMEM(block, BF16),
            pltpu.VMEM((n_y, n_z, OWN, LANES), BF16),
            pltpu.VMEM((n_y, n_z, OWN, LANES), BF16),
            pltpu.VMEM(block, BF16),
            pltpu.VMEM(block, BF16),
            pltpu.VMEM((n_z, n_y, OWN, LANES), BF16),
            pltpu.VMEM((2, 256, LANES), F32),
            pltpu.VMEM((2, 256, LANES), F32),
            pltpu.VMEM((n_dp * OWN, LANES), F32),
            pltpu.VMEM((OWN, 8 * HOP, SPAN), BF16),
            pltpu.VMEM((OWN, SPAN, SPAN), BF16),
            pltpu.VMEM((OWN, SPAN, SPAN), BF16),
            pltpu.VMEM((OWN * HOP, SPAN), F32),
            pltpu.VMEM((2, 2, 128, LANES), F32),
            pltpu.VMEM((8, 2, 16, 256), BF16),
            pltpu.VMEM((OWN * HOP, SPAN), F32),
            pltpu.VMEM((OWN, 8 * HOP, SPAN), BF16),
            pltpu.VMEM((OWN, 4, 8 * HOP, LANES), F32),
            pltpu.VMEM((n_dp * OWN, LANES), F32),
            pltpu.VMEM(filters.shape, BF16),
        ]
        + [pltpu.SemaphoreType.REGULAR] * 2
        + [pltpu.SemaphoreType.DMA((5,))]
        + [pltpu.SemaphoreType.DMA, pltpu.SemaphoreType.DMA((2,))]
        + [pltpu.SemaphoreType.DMA] * 10,
        compiler_params=pltpu.CompilerParams(collective_id=0, has_side_effects=True, vmem_limit_bytes=grant),
    )(
        upstream.reshape(rows, width),
        gate_value.reshape(rows, width),
        conv_input.reshape(rows, width),
        filters,
        skip_gain,
    )
    out, grad = pl.pallas_call(
        finish_kernel,
        out_shape=(jax.ShapeDtypeStruct((rows, width), BF16), jax.ShapeDtypeStruct(filters.shape, F32)),
        in_specs=[pl.BlockSpec(memory_space=pltpu.VMEM)] * 2,
        out_specs=[hbm] * 2,
        scratch_shapes=[
            pltpu.VMEM((rows, width), F32),
            pltpu.VMEM((rows, width), BF16),
            pltpu.VMEM(filters.shape, F32),
            pltpu.SemaphoreType.DMA((2,)),
        ],
        compiler_params=pltpu.CompilerParams(vmem_limit_bytes=16 * 1024 * 1024),
    )(back, grads)
    return out.reshape(upstream.shape), grad


def solution(mesh):
    in_specs = (
        P("ctx", None, "dp"),
        P("ctx", None, "dp"),
        P("ctx", None, "dp"),
        P(None, "ctx", "dp"),
        P("dp"),
    )
    out_specs = (P("ctx", None, "dp"), P(None, "ctx", "dp"))
    return jax.shard_map(body, mesh=mesh, in_specs=in_specs, out_specs=out_specs, check_vma=False)
```

```python
import functools

import jax
import jax.numpy as jnp
from jax import lax
from jax.experimental import pallas as pl
from jax.experimental.pallas import tpu as pltpu
from jax.sharding import PartitionSpec as P

MESH = pl.DeviceIdType.MESH
F32 = jnp.float32
BF16 = jnp.bfloat16

SPAN = 512
HOP = 16
LANES = 128
OWN = 8
SEQ = 2
FIRST = 1
LINE = 8


def lane_index(shape):
    return lax.broadcasted_iota(jnp.int32, shape, len(shape) - 1)


def row_index(shape):
    return lax.broadcasted_iota(jnp.int32, shape, len(shape) - 2)


def swap_groups(blocks):
    blocks = list(blocks)
    lane = lane_index((HOP, LANES)) // HOP
    for bit in (1, 2, 4):
        upper = (lane & bit) != 0
        for r in range(8):
            if r & bit:
                continue
            low, high = blocks[r], blocks[r | bit]
            blocks[r] = jnp.where(upper, pltpu.roll(high, HOP * bit, 1), low)
            blocks[r | bit] = jnp.where(upper, high, pltpu.roll(low, LANES - HOP * bit, 1))
    return blocks


def spread_rows(wide_ref, send_ref):
    halves = []
    for s in range(SEQ):
        part = wide_ref[pl.ds(s, 256, stride=2), :]
        halves.append(part.T.reshape(16, OWN, 256))
    send_ref[...] = jnp.concatenate(halves, axis=1).astype(BF16)


def build_toeplitz(hwide_ref, toep_ref, c):
    tiles = [hwide_ref[pl.ds(OWN * h + c, 8, stride=32), :] for h in range(4)]
    before = jnp.where(row_index((8, LANES)) == 0, 0.0, pltpu.roll(tiles[3], 1, 0))
    tiles = [before] + tiles
    keep = lane_index((HOP, LANES)) >= row_index((HOP, LANES))
    for q in range(8):
        turned = [
            pltpu.roll(jnp.broadcast_to(tile[q : q + 1, :], (HOP, LANES)), 0, 1, stride=1, stride_axis=0)
            for tile in tiles
        ]
        rows = [jnp.where(keep, turned[h + 1], turned[h]) for h in range(4)]
        toep_ref[c, q * HOP : (q + 1) * HOP, :] = jnp.concatenate(rows, axis=1).astype(BF16)


def own_rows(wide_ref, c):
    seqs = []
    for s in range(SEQ):
        seqs.append(
            jnp.concatenate(
                [
                    wide_ref[v, pl.ds(h * 16 + s * OWN + c, 8, stride=32), :]
                    for h in range(2)
                    for v in range(2)
                ],
                axis=1,
            )
        )
    return jnp.concatenate(seqs, axis=0)


def build_windows(gwide_ref, win_ref, c):
    here = own_rows(gwide_ref, c)
    after = pltpu.roll(here, 15, 0)
    after = jnp.where(row_index((16, SPAN)) % 8 == 7, 0.0, after)
    both = jnp.concatenate([here, after], axis=1)
    for r in range(8):
        turned = both if r == 0 else pltpu.roll(both, 2 * SPAN - HOP * r, 1)
        for jt in range(4):
            j = 8 * jt + r
            win_ref[c, j * 16 : (j + 1) * 16, :] = turned[:, LANES * jt : LANES * jt + SPAN].astype(BF16)


def back_rows(toep_ref, wint_ref, yall_ref, c, h):
    out = jnp.dot(toep_ref[c], wint_ref[c, :, 256 * h : 256 * h + 256], preferred_element_type=F32)
    group = lane_index((HOP, LANES)) % 8
    for n in range(2):
        tile = out[:, n * LANES : (n + 1) * LANES]
        total = tile[0:HOP]
        for q in range(1, 8):
            turned = pltpu.roll(tile[q * HOP : (q + 1) * HOP], LANES - q, 1)
            total = total + jnp.where(group < 8 - q, turned, 0.0)
        yall_ref[c * HOP : (c + 1) * HOP, 256 * h + n * LANES : 256 * h + (n + 1) * LANES] = total


def finish_back(yall_ref, gwide_ref, gain_ref, first_gain, ywide_ref, ysend_ref, h):
    cols = []
    for n in (2 * h, 2 * h + 1):
        turned = yall_ref[:, n * LANES : (n + 1) * LANES].T
        cols.append(swap_groups([turned[HOP * r : HOP * (r + 1)] for r in range(8)]))
    for c in range(OWN):
        gain = gain_ref[first_gain + c]
        for v in range(2):
            for s in range(SEQ):
                rows = cols[v][c][8 * s : 8 * s + 8]
                here = gwide_ref[v, pl.ds(h * 16 + s * OWN + c, 8, stride=32), :]
                ywide_ref[v, pl.ds(s * OWN + c, 8, stride=16), :] = rows + gain * here
    for v in range(2):
        ysend_ref[:, h, :, v * LANES : (v + 1) * LANES] = ywide_ref[v].reshape(8, 16, LANES).astype(BF16)


def turn_inputs(xwide_ref, xall_ref):
    rows = [own_rows(xwide_ref, c) for c in range(OWN)]
    for n in range(4):
        blocks = swap_groups([row[:, n * LANES : (n + 1) * LANES] for row in rows])
        xall_ref[:, n * LANES : (n + 1) * LANES] = jnp.concatenate(blocks, axis=0).T


def shift_inputs(xall_ref, xs_ref, c):
    group = lane_index((HOP, LANES)) % 8
    for n in range(4):
        tile = xall_ref[c * HOP : (c + 1) * HOP, n * LANES : (n + 1) * LANES].astype(BF16)
        for q in range(8):
            turned = tile if q == 0 else jnp.where(group >= q, pltpu.roll(tile, q, 1), jnp.zeros_like(tile))
            xs_ref[c, q * HOP : (q + 1) * HOP, n * LANES : (n + 1) * LANES] = turned


def filter_rows(xs_ref, win_ref, sums_ref, dwide_ref, c):
    out = jnp.dot(xs_ref[c], win_ref[c], preferred_element_type=F32)
    for n in range(4):
        sums_ref[c, n] = out[:, n * LANES : (n + 1) * LANES]
    lane = lane_index((8, LANES))
    rows = [[sums_ref[c, n, pl.ds(a, 8, stride=HOP), :] for n in range(4)] for a in range(HOP)]
    sums = rows[0]
    wrapped = jnp.zeros((8, LANES), F32)
    for a in range(1, HOP):
        turned = [pltpu.roll(row, LANES - a, 1) for row in rows[a]]
        inside = lane < LANES - a
        for n in range(3):
            sums[n] = sums[n] + jnp.where(inside, turned[n], turned[n + 1])
        sums[3] = sums[3] + jnp.where(inside, turned[3], 0.0)
        wrapped = wrapped + jnp.where(inside, 0.0, turned[0])
    wrapped = jnp.where(row_index((8, LANES)) == 7, 0.0, pltpu.roll(wrapped, 7, 0))
    sums[3] = sums[3] + wrapped
    for h in range(4):
        dwide_ref[pl.ds(OWN * h + c, 8, stride=32), :] = sums[h] * (1.0 / SEQ)


def widen(ref, wide_ref):
    for v in range(2):
        wide_ref[v] = ref[:, :, v * LANES : (v + 1) * LANES].astype(F32).reshape(256, LANES)


def kernel(
    n_ctx, n_dp, n_y,
    up_ref, gate_ref, in_ref, filt_ref, gain_ref,
    yrecv, drecv,
    up, gate, raw, filt, gain, wide, gsend, xsend, hsend, hpass, grecv, xrecv, hrecv, gwide, xwide, hwide, toep, win, wint,
    yall, ywide, ysend, xall, xs, sums, dwide, dsend,
    hello, hello_z, load_sem,
    h_send_sem, h_recv_sem, t_send_sem, t_recv_sem, g_send_sem, g_recv_sem, x_send_sem, x_recv_sem,
    y_send_sem, y_recv_sem, d_send_sem, d_recv_sem,
):
    me_ctx = lax.axis_index("ctx")
    me_dp = lax.axis_index("dp")
    half = n_ctx // 2
    me_hi = me_ctx // half
    me_lo = lax.rem(me_ctx, half)
    n_z = n_dp // n_y
    me_z = me_dp // n_y
    me_y = lax.rem(me_dp, n_y)

    def far_ctx(step):
        peer = (1 - me_hi) * half + lax.rem(me_lo + step, half)
        return peer, {"ctx": peer, "dp": me_dp}

    def first_far(step):
        peer = (1 - me_hi) * half + FIRST
        return peer, {"ctx": peer, "dp": me_dp}

    def other_far(step):
        peer = (1 - me_hi) * half + lax.rem(FIRST + 1 + lax.rem(me_lo + step, half - 1), half)
        return peer, {"ctx": peer, "dp": me_dp}

    def near_ctx(step):
        peer = me_hi * half + lax.rem(me_lo + step, half)
        return peer, {"ctx": peer, "dp": me_dp}

    def over_dp(step):
        peer = lax.rem(me_dp + step, n_dp)
        return peer, {"ctx": me_ctx, "dp": peer}

    def to_dp(peer):
        return peer, {"ctx": me_ctx, "dp": peer}

    def over_y(step):
        peer = lax.rem(me_y + step, n_y)
        return peer, {"ctx": me_ctx, "dp": me_z * n_y + peer}

    def over_z(step):
        peer = lax.rem(me_z + step, n_z)
        return peer, {"ctx": me_ctx, "dp": peer * n_y + me_y}

    def pieces(src, dst, sem, count):
        size = dst.shape[0] // count
        return [
            pltpu.make_async_copy(src.at[pl.ds(n * size, size)], dst.at[pl.ds(n * size, size)], sem)
            for n in range(count)
        ]

    def load(n, src, dst, count=4):
        for piece in pieces(src, dst, load_sem.at[n], count):
            piece.start()

    def loaded(n, dst):
        pltpu.make_async_copy(dst, dst, load_sem.at[n]).wait()

    load(0, up_ref, up)
    load(1, gate_ref, gate)
    barrier = pltpu.get_barrier_semaphore()

    def greet(first, last, over):
        @pl.loop(first, last)
        def _(step):
            pl.semaphore_signal(barrier, inc=1, device_id=over(step)[1], device_id_type=MESH)

    greet(0, half, far_ctx)
    def edge(y):
        return jnp.minimum(y, n_y - y)

    def sooner(step):
        return edge(lax.rem(me_y + step, n_y)) < edge(me_y)

    @pl.when(me_hi == 0)
    def _():
        greet(1, n_dp, over_dp)

    @pl.when(me_hi == 1)
    def _():
        greet(1, 3, over_y)
        greet(n_y - 2, n_y, over_y)
        for step in range(3, n_y - 2):
            peer, where = over_y(step)

            @pl.when(edge(me_y) < edge(peer))
            def _():
                pl.semaphore_signal(barrier, inc=1, device_id=where, device_id_type=MESH)

        for z in range(n_z):
            where = {"ctx": me_ctx, "dp": z * n_y + me_y}

            @pl.when(jnp.logical_and(z >= me_z - 1, z != me_z))
            def _():
                pl.semaphore_signal(barrier, inc=1, device_id=where, device_id_type=MESH)

    heard = 4 + me_z + jnp.where(me_z < n_z - 1, 1, 0)
    for step in range(3, n_y - 2):
        heard = heard + jnp.where(sooner(step), 1, 0)
    greeted = n_ctx - 1 + jnp.where(me_hi == 1, heard, n_dp - 1)

    greet(1, half, near_ctx)

    def scatter(first, last, over, me, src, dst, send_sem, recv_sem):
        @pl.loop(first, last)
        def _(step):
            peer, where = over(step)
            pltpu.make_async_remote_copy(
                src_ref=src.at[peer], dst_ref=dst.at[me], send_sem=send_sem, recv_sem=recv_sem,
                device_id=where, device_id_type=MESH,
            ).start()

    def keep_own(me, src, dst, recv_sem):
        pltpu.make_async_copy(src.at[me], dst.at[me], recv_sem).start()

    def pass_on(origin, src):
        pltpu.make_async_copy(src.at[origin, me_z], hrecv.at[me_z, origin], t_recv_sem).start()

        @pl.loop(1, n_z)
        def _(step):
            peer, where = over_z(step)
            pltpu.make_async_remote_copy(
                src_ref=src.at[origin, peer], dst_ref=hrecv.at[me_z, origin], send_sem=t_send_sem,
                recv_sem=t_recv_sem, device_id=where, device_id_type=MESH,
            ).start()

    def arrive(dst, sem):
        pltpu.make_async_copy(dst, dst, sem).wait()

    def sent(count, src, sem):
        part = src.at[pl.ds(0, count - 1)]
        pltpu.make_async_copy(part, part, sem).wait()

    load(2, in_ref, raw)
    load(3, filt_ref, filt)
    load(4, gain_ref, gain, 1)
    loaded(0, up)
    loaded(1, gate)
    wide[...] = (up[...].astype(F32) * gate[...].astype(F32)).astype(BF16).astype(F32)
    spread_rows(wide, gsend)
    loaded(2, raw)
    wide[...] = raw[...].astype(F32)
    spread_rows(wide, xsend)
    pl.semaphore_wait(barrier, greeted)
    scatter(0, 1, first_far, me_ctx, gsend, grecv, g_send_sem, g_recv_sem)

    @pl.when(me_hi == 1)
    def _():
        scatter(0, 1, first_far, me_ctx, xsend, xrecv, x_send_sem, x_recv_sem)

    scatter(0, half - 1, other_far, me_ctx, gsend, grecv, g_send_sem, g_recv_sem)
    @pl.when(me_hi == 1)
    def _():
        for step in (2, n_y - 2):
            pl.semaphore_signal(hello, inc=1, device_id=over_y(step)[1], device_id_type=MESH)
        for z in range(n_z - 2):

            @pl.when(z < me_z - 1)
            def _():
                pl.semaphore_signal(
                    hello_z, inc=1, device_id={"ctx": me_ctx, "dp": z * n_y + me_y}, device_id_type=MESH
                )

    loaded(3, filt)
    for z in range(n_z):
        hsend[:, z] = filt[z * n_y : (z + 1) * n_y].astype(BF16)
    @pl.when(me_hi == 0)
    def _():
        pltpu.make_async_copy(hsend.at[me_y, me_z], hrecv.at[me_z, me_y], t_recv_sem).start()

        @pl.loop(1, n_dp)
        def _(step):
            peer, where = over_dp(step)
            pltpu.make_async_remote_copy(
                src_ref=hsend.at[lax.rem(peer, n_y), peer // n_y], dst_ref=hrecv.at[me_z, me_y],
                send_sem=t_send_sem, recv_sem=t_recv_sem, device_id=where, device_id_type=MESH,
            ).start()

    @pl.when(me_hi == 1)
    def _():
        scatter(1, 3, over_y, me_y, hsend, hpass, h_send_sem, h_recv_sem.at[0])
        scatter(n_y - 2, n_y, over_y, me_y, hsend, hpass, h_send_sem, h_recv_sem.at[0])
        for step in range(3, n_y - 2):

            @pl.when(sooner(step))
            def _():
                scatter(step, step + 1, over_y, me_y, hsend, hpass, h_send_sem, h_recv_sem.at[1])


    @pl.when(me_hi == 1)
    def _():
        scatter(0, half - 1, other_far, me_ctx, xsend, xrecv, x_send_sem, x_recv_sem)

    scatter(1, half, near_ctx, me_ctx, gsend, grecv, g_send_sem, g_recv_sem)
    scatter(1, half, near_ctx, me_ctx, xsend, xrecv, x_send_sem, x_recv_sem)
    keep_own(me_ctx, gsend, grecv, g_recv_sem)
    keep_own(me_ctx, xsend, xrecv, x_recv_sem)
    loaded(4, gain)
    @pl.when(me_hi == 1)
    def _():
        pl.semaphore_wait(hello, 2)
        for step in range(3, n_y - 2):

            @pl.when(jnp.logical_not(sooner(step)))
            def _():
                scatter(step, step + 1, over_y, me_y, hsend, hpass, h_send_sem, h_recv_sem.at[1])


        for z in range(n_z - 2):

            @pl.when(z == me_z)
            def _():
                pl.semaphore_wait(hello_z, n_z - 2 - z)

        pass_on(me_y, hsend)
        arrive(hpass.at[pl.ds(0, 4)], h_recv_sem.at[0])
        for step in (1, n_y - 1, 2, n_y - 2):
            pass_on(lax.rem(me_y + step, n_y), hpass)
        arrive(hpass.at[pl.ds(0, n_y - 5)], h_recv_sem.at[1])
        for step in range(3, n_y - 2):
            pass_on(lax.rem(me_y + step, n_y), hpass)

    arrive(grecv, g_recv_sem)

    @pl.when(me_hi == 0)
    def _():
        scatter(0, half, far_ctx, me_ctx, xsend, xrecv, x_send_sem, x_recv_sem)

    widen(grecv, gwide)
    for c in range(OWN):
        build_windows(gwide, win, c)
    for c in range(OWN):
        wint[c] = win[c].T

    @pl.loop(0, 2)
    def _(turn):
        @pl.when(turn != me_hi)
        def _():
            arrive(hrecv, t_recv_sem)
            hwide[...] = hrecv[...].astype(F32).reshape(n_dp * OWN, LANES)
            for c in range(OWN):
                build_toeplitz(hwide, toep, c)

            for h in (1, 0):
                for c in range(OWN):
                    back_rows(toep, wint, yall, c, h)
                finish_back(yall, gwide, gain, me_ctx * OWN, ywide.at[h], ysend, h)

                @pl.loop(0, n_ctx // 2)
                def _(step):
                    block = half // 2 * (step // (half // 2)) + lax.rem(me_lo // 2 + step, half // 2)
                    peer = 2 * block + h

                    @pl.when(peer != me_ctx)
                    def _():
                        pltpu.make_async_remote_copy(
                            src_ref=ysend.at[block, h], dst_ref=yrecv.at[me_ctx], send_sem=y_send_sem,
                            recv_sem=y_recv_sem, device_id={"ctx": peer, "dp": me_dp}, device_id_type=MESH,
                        ).start()

                    @pl.when(peer == me_ctx)
                    def _():
                        pltpu.make_async_copy(ysend.at[block, h], yrecv.at[me_ctx], y_recv_sem).start()

        @pl.when(turn == me_hi)
        def _():
            arrive(xrecv, x_recv_sem)
            widen(xrecv, xwide)
            turn_inputs(xwide, xall)
            for c in range(OWN):
                shift_inputs(xall, xs, c)
            for c in range(OWN):
                filter_rows(xs, win, sums, dwide, c)
            dsend[...] = dwide[...].reshape(n_dp, OWN, LANES).astype(BF16)
            scatter(0, me_dp, to_dp, me_dp, dsend, drecv, d_send_sem, d_recv_sem)
            scatter(me_dp + 1, n_dp, to_dp, me_dp, dsend, drecv, d_send_sem, d_recv_sem)
            keep_own(me_dp, dsend, drecv, d_recv_sem)

    @pl.when(me_hi == 0)
    def _():
        sent(n_dp, hrecv.reshape(n_dp, OWN, LANES), t_send_sem)

    @pl.when(me_hi == 1)
    def _():
        sent(n_y, hsend, h_send_sem)
        sent(n_z, hrecv, t_send_sem)

    sent(n_ctx, gsend, g_send_sem)
    sent(n_ctx, xsend, x_send_sem)
    sent(n_ctx, yrecv, y_send_sem)
    sent(n_dp, dsend, d_send_sem)
    arrive(yrecv, y_recv_sem)
    arrive(drecv, d_recv_sem)


def finish_kernel(y_in, d_in, out_ref, grad_ref, wide, out, grad, store_sem):
    def store(n, src, dst, first, size):
        part = pl.ds(first, size)
        pltpu.make_async_copy(src.at[part], dst.at[part], store_sem.at[n]).start()

    for n in range(4):
        grad[8 * n : 8 * n + 8] = d_in[8 * n : 8 * n + 8].astype(F32)
        store(0, grad, grad_ref, 8 * n, 8)
    for n in range(2):
        time = slice(n * LANES, (n + 1) * LANES)
        back = y_in[:, :, time].astype(F32)
        for s in range(SEQ):
            wide[pl.ds(256 * n + s, LANES, stride=2), :] = (
                back[:, s * OWN : (s + 1) * OWN, :].reshape(16 * OWN, LANES).T
            )
        out[256 * n : 256 * n + 256] = wide[256 * n : 256 * n + 256].astype(BF16)
        for k in range(2):
            store(1, out, out_ref, 256 * n + 128 * k, 128)
    pltpu.make_async_copy(grad, grad_ref, store_sem.at[0]).wait()
    pltpu.make_async_copy(out, out_ref, store_sem.at[1]).wait()


def body(upstream, gate_value, conv_input, filters, skip_gain):
    n_ctx = lax.axis_size("ctx")
    n_dp = lax.axis_size("dp")
    n_y = LINE
    n_z = n_dp // n_y
    rows = upstream.shape[0] * upstream.shape[1]
    width = upstream.shape[2]
    block = (16, 16, 256)
    hbm = pl.BlockSpec(memory_space=pltpu.HBM)
    grant = 56 * 1024 * 1024
    back, grads = pl.pallas_call(
        functools.partial(kernel, n_ctx, n_dp, n_y),
        out_shape=(pltpu.VMEM(block, BF16), pltpu.VMEM(filters.shape, BF16)),
        in_specs=[hbm] * 5,
        out_specs=[pl.BlockSpec(memory_space=pltpu.VMEM)] * 2,
        scratch_shapes=[
            pltpu.VMEM((rows, width), BF16),
            pltpu.VMEM((rows, width), BF16),
            pltpu.VMEM((rows, width), BF16),
            pltpu.VMEM(filters.shape, F32),
            pltpu.SMEM(skip_gain.shape, F32),
            pltpu.VMEM((rows, width), F32),
            pltpu.VMEM(block, BF16),
            pltpu.VMEM(block, BF16),
            pltpu.VMEM((n_y, n_z, OWN, LANES), BF16),
            pltpu.VMEM((n_y, n_z, OWN, LANES), BF16),
            pltpu.VMEM(block, BF16),
            pltpu.VMEM(block, BF16),
            pltpu.VMEM((n_z, n_y, OWN, LANES), BF16),
            pltpu.VMEM((2, 256, LANES), F32),
            pltpu.VMEM((2, 256, LANES), F32),
            pltpu.VMEM((n_dp * OWN, LANES), F32),
            pltpu.VMEM((OWN, 8 * HOP, SPAN), BF16),
            pltpu.VMEM((OWN, SPAN, SPAN), BF16),
            pltpu.VMEM((OWN, SPAN, SPAN), BF16),
            pltpu.VMEM((OWN * HOP, SPAN), F32),
            pltpu.VMEM((2, 2, 128, LANES), F32),
            pltpu.VMEM((8, 2, 16, 256), BF16),
            pltpu.VMEM((OWN * HOP, SPAN), F32),
            pltpu.VMEM((OWN, 8 * HOP, SPAN), BF16),
            pltpu.VMEM((OWN, 4, 8 * HOP, LANES), F32),
            pltpu.VMEM((n_dp * OWN, LANES), F32),
            pltpu.VMEM(filters.shape, BF16),
        ]
        + [pltpu.SemaphoreType.REGULAR] * 2
        + [pltpu.SemaphoreType.DMA((5,))]
        + [pltpu.SemaphoreType.DMA, pltpu.SemaphoreType.DMA((2,))]
        + [pltpu.SemaphoreType.DMA] * 10,
        compiler_params=pltpu.CompilerParams(collective_id=0, has_side_effects=True, vmem_limit_bytes=grant),
    )(
        upstream.reshape(rows, width),
        gate_value.reshape(rows, width),
        conv_input.reshape(rows, width),
        filters,
        skip_gain,
    )
    out, grad = pl.pallas_call(
        finish_kernel,
        out_shape=(jax.ShapeDtypeStruct((rows, width), BF16), jax.ShapeDtypeStruct(filters.shape, F32)),
        in_specs=[pl.BlockSpec(memory_space=pltpu.VMEM)] * 2,
        out_specs=[hbm] * 2,
        scratch_shapes=[
            pltpu.VMEM((rows, width), F32),
            pltpu.VMEM((rows, width), BF16),
            pltpu.VMEM(filters.shape, F32),
            pltpu.SemaphoreType.DMA((2,)),
        ],
        compiler_params=pltpu.CompilerParams(vmem_limit_bytes=16 * 1024 * 1024),
    )(back, grads)
    return out.reshape(upstream.shape), grad


def solution(mesh):
    in_specs = (
        P("ctx", None, "dp"),
        P("ctx", None, "dp"),
        P("ctx", None, "dp"),
        P(None, "ctx", "dp"),
        P("dp"),
    )
    out_specs = (P("ctx", None, "dp"), P(None, "ctx", "dp"))
    return jax.shard_map(body, mesh=mesh, in_specs=in_specs, out_specs=out_specs, check_vma=False)
```

```python
import functools

import jax
import jax.numpy as jnp
from jax import lax
from jax.experimental import pallas as pl
from jax.experimental.pallas import tpu as pltpu
from jax.sharding import PartitionSpec as P

MESH = pl.DeviceIdType.MESH
F32 = jnp.float32
BF16 = jnp.bfloat16

SPAN = 512
HOP = 16
LANES = 128
OWN = 8
SEQ = 2
FIRST = 1
LINE = 8


def lane_index(shape):
    return lax.broadcasted_iota(jnp.int32, shape, len(shape) - 1)


def row_index(shape):
    return lax.broadcasted_iota(jnp.int32, shape, len(shape) - 2)


def swap_groups(blocks):
    blocks = list(blocks)
    lane = lane_index((HOP, LANES)) // HOP
    for bit in (1, 2, 4):
        upper = (lane & bit) != 0
        for r in range(8):
            if r & bit:
                continue
            low, high = blocks[r], blocks[r | bit]
            blocks[r] = jnp.where(upper, pltpu.roll(high, HOP * bit, 1), low)
            blocks[r | bit] = jnp.where(upper, high, pltpu.roll(low, LANES - HOP * bit, 1))
    return blocks


def spread_rows(wide_ref, send_ref):
    halves = []
    for s in range(SEQ):
        part = wide_ref[pl.ds(s, 256, stride=2), :]
        halves.append(part.T.reshape(16, OWN, 256))
    send_ref[...] = jnp.concatenate(halves, axis=1).astype(BF16)


def build_toeplitz(hwide_ref, toep_ref, c):
    tiles = [hwide_ref[pl.ds(OWN * h + c, 8, stride=32), :] for h in range(4)]
    before = jnp.where(row_index((8, LANES)) == 0, 0.0, pltpu.roll(tiles[3], 1, 0))
    tiles = [before] + tiles
    keep = lane_index((HOP, LANES)) >= row_index((HOP, LANES))
    for q in range(8):
        turned = [
            pltpu.roll(jnp.broadcast_to(tile[q : q + 1, :], (HOP, LANES)), 0, 1, stride=1, stride_axis=0)
            for tile in tiles
        ]
        rows = [jnp.where(keep, turned[h + 1], turned[h]) for h in range(4)]
        toep_ref[c, q * HOP : (q + 1) * HOP, :] = jnp.concatenate(rows, axis=1).astype(BF16)


def own_rows(wide_ref, c):
    seqs = []
    for s in range(SEQ):
        seqs.append(
            jnp.concatenate(
                [
                    wide_ref[v, pl.ds(h * 16 + s * OWN + c, 8, stride=32), :]
                    for h in range(2)
                    for v in range(2)
                ],
                axis=1,
            )
        )
    return jnp.concatenate(seqs, axis=0)


def build_windows(gwide_ref, win_ref, c):
    here = own_rows(gwide_ref, c)
    after = pltpu.roll(here, 15, 0)
    after = jnp.where(row_index((16, SPAN)) % 8 == 7, 0.0, after)
    both = jnp.concatenate([here, after], axis=1)
    for r in range(8):
        turned = both if r == 0 else pltpu.roll(both, 2 * SPAN - HOP * r, 1)
        for jt in range(4):
            j = 8 * jt + r
            win_ref[c, j * 16 : (j + 1) * 16, :] = turned[:, LANES * jt : LANES * jt + SPAN].astype(BF16)


def back_rows(toep_ref, wint_ref, yall_ref, c, h):
    out = jnp.dot(toep_ref[c], wint_ref[c, :, 256 * h : 256 * h + 256], preferred_element_type=F32)
    group = lane_index((HOP, LANES)) % 8
    for n in range(2):
        tile = out[:, n * LANES : (n + 1) * LANES]
        total = tile[0:HOP]
        for q in range(1, 8):
            turned = pltpu.roll(tile[q * HOP : (q + 1) * HOP], LANES - q, 1)
            total = total + jnp.where(group < 8 - q, turned, 0.0)
        yall_ref[c * HOP : (c + 1) * HOP, 256 * h + n * LANES : 256 * h + (n + 1) * LANES] = total


def finish_back(yall_ref, gwide_ref, gain_ref, first_gain, ywide_ref, ysend_ref, h):
    cols = []
    for n in (2 * h, 2 * h + 1):
        turned = yall_ref[:, n * LANES : (n + 1) * LANES].T
        cols.append(swap_groups([turned[HOP * r : HOP * (r + 1)] for r in range(8)]))
    for c in range(OWN):
        gain = gain_ref[first_gain + c]
        for v in range(2):
            for s in range(SEQ):
                rows = cols[v][c][8 * s : 8 * s + 8]
                here = gwide_ref[v, pl.ds(h * 16 + s * OWN + c, 8, stride=32), :]
                ywide_ref[v, pl.ds(s * OWN + c, 8, stride=16), :] = rows + gain * here
    for v in range(2):
        ysend_ref[:, h, :, v * LANES : (v + 1) * LANES] = ywide_ref[v].reshape(8, 16, LANES).astype(BF16)


def turn_inputs(xwide_ref, xall_ref):
    rows = [own_rows(xwide_ref, c) for c in range(OWN)]
    for n in range(4):
        blocks = swap_groups([row[:, n * LANES : (n + 1) * LANES] for row in rows])
        xall_ref[:, n * LANES : (n + 1) * LANES] = jnp.concatenate(blocks, axis=0).T


def shift_inputs(xall_ref, xs_ref, c):
    group = lane_index((HOP, LANES)) % 8
    for n in range(4):
        tile = xall_ref[c * HOP : (c + 1) * HOP, n * LANES : (n + 1) * LANES].astype(BF16)
        for q in range(8):
            turned = tile if q == 0 else jnp.where(group >= q, pltpu.roll(tile, q, 1), jnp.zeros_like(tile))
            xs_ref[c, q * HOP : (q + 1) * HOP, n * LANES : (n + 1) * LANES] = turned


def filter_rows(xs_ref, win_ref, sums_ref, dwide_ref, c):
    out = jnp.dot(xs_ref[c], win_ref[c], preferred_element_type=F32)
    for n in range(4):
        sums_ref[c, n] = out[:, n * LANES : (n + 1) * LANES]
    lane = lane_index((8, LANES))
    rows = [[sums_ref[c, n, pl.ds(a, 8, stride=HOP), :] for n in range(4)] for a in range(HOP)]
    sums = rows[0]
    wrapped = jnp.zeros((8, LANES), F32)
    for a in range(1, HOP):
        turned = [pltpu.roll(row, LANES - a, 1) for row in rows[a]]
        inside = lane < LANES - a
        for n in range(3):
            sums[n] = sums[n] + jnp.where(inside, turned[n], turned[n + 1])
        sums[3] = sums[3] + jnp.where(inside, turned[3], 0.0)
        wrapped = wrapped + jnp.where(inside, 0.0, turned[0])
    wrapped = jnp.where(row_index((8, LANES)) == 7, 0.0, pltpu.roll(wrapped, 7, 0))
    sums[3] = sums[3] + wrapped
    for h in range(4):
        dwide_ref[pl.ds(OWN * h + c, 8, stride=32), :] = sums[h] * (1.0 / SEQ)


def widen(ref, wide_ref):
    for v in range(2):
        wide_ref[v] = ref[:, :, v * LANES : (v + 1) * LANES].astype(F32).reshape(256, LANES)


def kernel(
    n_ctx, n_dp, n_y,
    up_ref, gate_ref, in_ref, filt_ref, gain_ref,
    yrecv, drecv,
    up, gate, raw, filt, gain, wide, gsend, xsend, hsend, hpass, grecv, xrecv, hrecv, gwide, xwide, hwide, toep, win, wint,
    yall, ywide, ysend, xall, xs, sums, dwide, dsend,
    hello, hello_z, load_sem,
    h_send_sem, h_recv_sem, t_send_sem, t_recv_sem, g_send_sem, g_recv_sem, x_send_sem, x_recv_sem,
    y_send_sem, y_recv_sem, d_send_sem, d_recv_sem,
):
    me_ctx = lax.axis_index("ctx")
    me_dp = lax.axis_index("dp")
    half = n_ctx // 2
    me_hi = me_ctx // half
    me_lo = lax.rem(me_ctx, half)
    n_z = n_dp // n_y
    me_z = me_dp // n_y
    me_y = lax.rem(me_dp, n_y)

    def far_ctx(step):
        peer = (1 - me_hi) * half + lax.rem(me_lo + step, half)
        return peer, {"ctx": peer, "dp": me_dp}

    def first_far(step):
        peer = (1 - me_hi) * half + FIRST
        return peer, {"ctx": peer, "dp": me_dp}

    def other_far(step):
        peer = (1 - me_hi) * half + lax.rem(FIRST + 1 + lax.rem(me_lo + step, half - 1), half)
        return peer, {"ctx": peer, "dp": me_dp}

    def near_ctx(step):
        peer = me_hi * half + lax.rem(me_lo + step, half)
        return peer, {"ctx": peer, "dp": me_dp}

    def over_dp(step):
        peer = lax.rem(me_dp + step, n_dp)
        return peer, {"ctx": me_ctx, "dp": peer}

    def to_dp(peer):
        return peer, {"ctx": me_ctx, "dp": peer}

    def over_y(step):
        peer = lax.rem(me_y + step, n_y)
        return peer, {"ctx": me_ctx, "dp": me_z * n_y + peer}

    def over_z(step):
        peer = lax.rem(me_z + step, n_z)
        return peer, {"ctx": me_ctx, "dp": peer * n_y + me_y}

    def pieces(src, dst, sem, count):
        size = dst.shape[0] // count
        return [
            pltpu.make_async_copy(src.at[pl.ds(n * size, size)], dst.at[pl.ds(n * size, size)], sem)
            for n in range(count)
        ]

    def load(n, src, dst, count=4):
        for piece in pieces(src, dst, load_sem.at[n], count):
            piece.start()

    def loaded(n, dst):
        pltpu.make_async_copy(dst, dst, load_sem.at[n]).wait()

    load(0, up_ref, up)
    load(1, gate_ref, gate)
    barrier = pltpu.get_barrier_semaphore()

    def greet(first, last, over):
        @pl.loop(first, last)
        def _(step):
            pl.semaphore_signal(barrier, inc=1, device_id=over(step)[1], device_id_type=MESH)

    greet(0, half, far_ctx)
    def edge(y):
        return jnp.minimum(y, n_y - y)

    def sooner(step):
        return edge(lax.rem(me_y + step, n_y)) < edge(me_y)

    @pl.when(me_hi == 0)
    def _():
        greet(1, n_dp, over_dp)

    @pl.when(me_hi == 1)
    def _():
        greet(1, 3, over_y)
        greet(n_y - 2, n_y, over_y)
        for step in range(3, n_y - 2):
            peer, where = over_y(step)

            @pl.when(edge(me_y) < edge(peer))
            def _():
                pl.semaphore_signal(barrier, inc=1, device_id=where, device_id_type=MESH)

        for z in range(n_z):
            where = {"ctx": me_ctx, "dp": z * n_y + me_y}

            @pl.when(jnp.logical_and(z >= me_z - 1, z != me_z))
            def _():
                pl.semaphore_signal(barrier, inc=1, device_id=where, device_id_type=MESH)

    heard = 4 + me_z + jnp.where(me_z < n_z - 1, 1, 0)
    for step in range(3, n_y - 2):
        heard = heard + jnp.where(sooner(step), 1, 0)
    greeted = n_ctx - 1 + jnp.where(me_hi == 1, heard, n_dp - 1)

    greet(1, half, near_ctx)

    def scatter(first, last, over, me, src, dst, send_sem, recv_sem):
        @pl.loop(first, last)
        def _(step):
            peer, where = over(step)
            pltpu.make_async_remote_copy(
                src_ref=src.at[peer], dst_ref=dst.at[me], send_sem=send_sem, recv_sem=recv_sem,
                device_id=where, device_id_type=MESH,
            ).start()

    def keep_own(me, src, dst, recv_sem):
        pltpu.make_async_copy(src.at[me], dst.at[me], recv_sem).start()

    def pass_on(origin, src):
        pltpu.make_async_copy(src.at[origin, me_z], hrecv.at[me_z, origin], t_recv_sem).start()

        @pl.loop(1, n_z)
        def _(step):
            peer, where = over_z(step)
            pltpu.make_async_remote_copy(
                src_ref=src.at[origin, peer], dst_ref=hrecv.at[me_z, origin], send_sem=t_send_sem,
                recv_sem=t_recv_sem, device_id=where, device_id_type=MESH,
            ).start()

    def arrive(dst, sem):
        pltpu.make_async_copy(dst, dst, sem).wait()

    def sent(count, src, sem):
        part = src.at[pl.ds(0, count - 1)]
        pltpu.make_async_copy(part, part, sem).wait()

    load(2, in_ref, raw)
    load(3, filt_ref, filt)
    load(4, gain_ref, gain, 1)
    loaded(0, up)
    loaded(1, gate)
    wide[...] = (up[...].astype(F32) * gate[...].astype(F32)).astype(BF16).astype(F32)
    spread_rows(wide, gsend)
    loaded(2, raw)
    wide[...] = raw[...].astype(F32)
    spread_rows(wide, xsend)
    pl.semaphore_wait(barrier, greeted)
    scatter(0, 1, first_far, me_ctx, gsend, grecv, g_send_sem, g_recv_sem)

    @pl.when(me_hi == 1)
    def _():
        scatter(0, 1, first_far, me_ctx, xsend, xrecv, x_send_sem, x_recv_sem)

    scatter(0, half - 1, other_far, me_ctx, gsend, grecv, g_send_sem, g_recv_sem)
    @pl.when(me_hi == 1)
    def _():
        for step in (2, n_y - 2):
            pl.semaphore_signal(hello, inc=1, device_id=over_y(step)[1], device_id_type=MESH)
        for z in range(n_z - 2):

            @pl.when(z < me_z - 1)
            def _():
                pl.semaphore_signal(
                    hello_z, inc=1, device_id={"ctx": me_ctx, "dp": z * n_y + me_y}, device_id_type=MESH
                )

    loaded(3, filt)
    for z in range(n_z):
        hsend[:, z] = filt[z * n_y : (z + 1) * n_y].astype(BF16)
    @pl.when(me_hi == 0)
    def _():
        pltpu.make_async_copy(hsend.at[me_y, me_z], hrecv.at[me_z, me_y], t_recv_sem).start()

        @pl.loop(1, n_dp)
        def _(step):
            peer, where = over_dp(step)
            pltpu.make_async_remote_copy(
                src_ref=hsend.at[lax.rem(peer, n_y), peer // n_y], dst_ref=hrecv.at[me_z, me_y],
                send_sem=t_send_sem, recv_sem=t_recv_sem, device_id=where, device_id_type=MESH,
            ).start()

    @pl.when(me_hi == 1)
    def _():
        scatter(1, 3, over_y, me_y, hsend, hpass, h_send_sem, h_recv_sem.at[0])
        scatter(n_y - 2, n_y, over_y, me_y, hsend, hpass, h_send_sem, h_recv_sem.at[0])
        for step in range(3, n_y - 2):

            @pl.when(sooner(step))
            def _():
                scatter(step, step + 1, over_y, me_y, hsend, hpass, h_send_sem, h_recv_sem.at[1])


    @pl.when(me_hi == 1)
    def _():
        scatter(0, half - 1, other_far, me_ctx, xsend, xrecv, x_send_sem, x_recv_sem)

    scatter(1, half, near_ctx, me_ctx, gsend, grecv, g_send_sem, g_recv_sem)
    scatter(1, half, near_ctx, me_ctx, xsend, xrecv, x_send_sem, x_recv_sem)
    keep_own(me_ctx, gsend, grecv, g_recv_sem)
    keep_own(me_ctx, xsend, xrecv, x_recv_sem)
    loaded(4, gain)
    @pl.when(me_hi == 1)
    def _():
        pl.semaphore_wait(hello, 2)
        for step in range(3, n_y - 2):

            @pl.when(jnp.logical_not(sooner(step)))
            def _():
                scatter(step, step + 1, over_y, me_y, hsend, hpass, h_send_sem, h_recv_sem.at[1])


        for z in range(n_z - 2):

            @pl.when(z == me_z)
            def _():
                pl.semaphore_wait(hello_z, n_z - 2 - z)

        pass_on(me_y, hsend)
        arrive(hpass.at[pl.ds(0, 4)], h_recv_sem.at[0])
        for step in (1, n_y - 1, 2, n_y - 2):
            pass_on(lax.rem(me_y + step, n_y), hpass)
        arrive(hpass.at[pl.ds(0, n_y - 5)], h_recv_sem.at[1])
        for step in range(3, n_y - 2):
            pass_on(lax.rem(me_y + step, n_y), hpass)

    arrive(grecv, g_recv_sem)

    @pl.when(me_hi == 0)
    def _():
        scatter(0, half, far_ctx, me_ctx, xsend, xrecv, x_send_sem, x_recv_sem)

    widen(grecv, gwide)
    for c in range(OWN):
        build_windows(gwide, win, c)
    for c in range(OWN):
        wint[c] = win[c].T

    @pl.loop(0, 2)
    def _(turn):
        @pl.when(turn != me_hi)
        def _():
            arrive(hrecv, t_recv_sem)
            hwide[...] = hrecv[...].astype(F32).reshape(n_dp * OWN, LANES)
            for c in range(OWN):
                build_toeplitz(hwide, toep, c)

            for h in (1, 0):
                for c in range(OWN):
                    back_rows(toep, wint, yall, c, h)
                finish_back(yall, gwide, gain, me_ctx * OWN, ywide.at[h], ysend, h)

                @pl.loop(0, n_ctx // 2)
                def _(step):
                    block = step
                    peer = 2 * block + h

                    @pl.when(peer != me_ctx)
                    def _():
                        pltpu.make_async_remote_copy(
                            src_ref=ysend.at[block, h], dst_ref=yrecv.at[me_ctx], send_sem=y_send_sem,
                            recv_sem=y_recv_sem, device_id={"ctx": peer, "dp": me_dp}, device_id_type=MESH,
                        ).start()

                    @pl.when(peer == me_ctx)
                    def _():
                        pltpu.make_async_copy(ysend.at[block, h], yrecv.at[me_ctx], y_recv_sem).start()

        @pl.when(turn == me_hi)
        def _():
            arrive(xrecv, x_recv_sem)
            widen(xrecv, xwide)
            turn_inputs(xwide, xall)
            for c in range(OWN):
                shift_inputs(xall, xs, c)
            for c in range(OWN):
                filter_rows(xs, win, sums, dwide, c)
            dsend[...] = dwide[...].reshape(n_dp, OWN, LANES).astype(BF16)
            scatter(0, me_dp, to_dp, me_dp, dsend, drecv, d_send_sem, d_recv_sem)
            scatter(me_dp + 1, n_dp, to_dp, me_dp, dsend, drecv, d_send_sem, d_recv_sem)
            keep_own(me_dp, dsend, drecv, d_recv_sem)

    @pl.when(me_hi == 0)
    def _():
        sent(n_dp, hrecv.reshape(n_dp, OWN, LANES), t_send_sem)

    @pl.when(me_hi == 1)
    def _():
        sent(n_y, hsend, h_send_sem)
        sent(n_z, hrecv, t_send_sem)

    sent(n_ctx, gsend, g_send_sem)
    sent(n_ctx, xsend, x_send_sem)
    sent(n_ctx, yrecv, y_send_sem)
    sent(n_dp, dsend, d_send_sem)
    arrive(yrecv, y_recv_sem)
    arrive(drecv, d_recv_sem)


def finish_kernel(y_in, d_in, out_ref, grad_ref, wide, out, grad, store_sem):
    def store(n, src, dst, first, size):
        part = pl.ds(first, size)
        pltpu.make_async_copy(src.at[part], dst.at[part], store_sem.at[n]).start()

    for n in range(4):
        grad[8 * n : 8 * n + 8] = d_in[8 * n : 8 * n + 8].astype(F32)
        store(0, grad, grad_ref, 8 * n, 8)
    for n in range(2):
        time = slice(n * LANES, (n + 1) * LANES)
        back = y_in[:, :, time].astype(F32)
        for s in range(SEQ):
            wide[pl.ds(256 * n + s, LANES, stride=2), :] = (
                back[:, s * OWN : (s + 1) * OWN, :].reshape(16 * OWN, LANES).T
            )
        out[256 * n : 256 * n + 256] = wide[256 * n : 256 * n + 256].astype(BF16)
        for k in range(2):
            store(1, out, out_ref, 256 * n + 128 * k, 128)
    pltpu.make_async_copy(grad, grad_ref, store_sem.at[0]).wait()
    pltpu.make_async_copy(out, out_ref, store_sem.at[1]).wait()


def body(upstream, gate_value, conv_input, filters, skip_gain):
    n_ctx = lax.axis_size("ctx")
    n_dp = lax.axis_size("dp")
    n_y = LINE
    n_z = n_dp // n_y
    rows = upstream.shape[0] * upstream.shape[1]
    width = upstream.shape[2]
    block = (16, 16, 256)
    hbm = pl.BlockSpec(memory_space=pltpu.HBM)
    grant = 56 * 1024 * 1024
    back, grads = pl.pallas_call(
        functools.partial(kernel, n_ctx, n_dp, n_y),
        out_shape=(pltpu.VMEM(block, BF16), pltpu.VMEM(filters.shape, BF16)),
        in_specs=[hbm] * 5,
        out_specs=[pl.BlockSpec(memory_space=pltpu.VMEM)] * 2,
        scratch_shapes=[
            pltpu.VMEM((rows, width), BF16),
            pltpu.VMEM((rows, width), BF16),
            pltpu.VMEM((rows, width), BF16),
            pltpu.VMEM(filters.shape, F32),
            pltpu.SMEM(skip_gain.shape, F32),
            pltpu.VMEM((rows, width), F32),
            pltpu.VMEM(block, BF16),
            pltpu.VMEM(block, BF16),
            pltpu.VMEM((n_y, n_z, OWN, LANES), BF16),
            pltpu.VMEM((n_y, n_z, OWN, LANES), BF16),
            pltpu.VMEM(block, BF16),
            pltpu.VMEM(block, BF16),
            pltpu.VMEM((n_z, n_y, OWN, LANES), BF16),
            pltpu.VMEM((2, 256, LANES), F32),
            pltpu.VMEM((2, 256, LANES), F32),
            pltpu.VMEM((n_dp * OWN, LANES), F32),
            pltpu.VMEM((OWN, 8 * HOP, SPAN), BF16),
            pltpu.VMEM((OWN, SPAN, SPAN), BF16),
            pltpu.VMEM((OWN, SPAN, SPAN), BF16),
            pltpu.VMEM((OWN * HOP, SPAN), F32),
            pltpu.VMEM((2, 2, 128, LANES), F32),
            pltpu.VMEM((8, 2, 16, 256), BF16),
            pltpu.VMEM((OWN * HOP, SPAN), F32),
            pltpu.VMEM((OWN, 8 * HOP, SPAN), BF16),
            pltpu.VMEM((OWN, 4, 8 * HOP, LANES), F32),
            pltpu.VMEM((n_dp * OWN, LANES), F32),
            pltpu.VMEM(filters.shape, BF16),
        ]
        + [pltpu.SemaphoreType.REGULAR] * 2
        + [pltpu.SemaphoreType.DMA((5,))]
        + [pltpu.SemaphoreType.DMA, pltpu.SemaphoreType.DMA((2,))]
        + [pltpu.SemaphoreType.DMA] * 10,
        compiler_params=pltpu.CompilerParams(collective_id=0, has_side_effects=True, vmem_limit_bytes=grant),
    )(
        upstream.reshape(rows, width),
        gate_value.reshape(rows, width),
        conv_input.reshape(rows, width),
        filters,
        skip_gain,
    )
    out, grad = pl.pallas_call(
        finish_kernel,
        out_shape=(jax.ShapeDtypeStruct((rows, width), BF16), jax.ShapeDtypeStruct(filters.shape, F32)),
        in_specs=[pl.BlockSpec(memory_space=pltpu.VMEM)] * 2,
        out_specs=[hbm] * 2,
        scratch_shapes=[
            pltpu.VMEM((rows, width), F32),
            pltpu.VMEM((rows, width), BF16),
            pltpu.VMEM(filters.shape, F32),
            pltpu.SemaphoreType.DMA((2,)),
        ],
        compiler_params=pltpu.CompilerParams(vmem_limit_bytes=16 * 1024 * 1024),
    )(back, grads)
    return out.reshape(upstream.shape), grad


def solution(mesh):
    in_specs = (
        P("ctx", None, "dp"),
        P("ctx", None, "dp"),
        P("ctx", None, "dp"),
        P(None, "ctx", "dp"),
        P("dp"),
    )
    out_specs = (P("ctx", None, "dp"), P(None, "ctx", "dp"))
    return jax.shard_map(body, mesh=mesh, in_specs=in_specs, out_specs=out_specs, check_vma=False)
```
